128 devices in a mesh: row: 16 (over z_lo, x, core), col: 8 (over z_hi, y).
Axes of the slice: x: 4, y: 4, z: 4 (z_hi: 2, z_lo: 2; z = z_hi * 2 + z_lo), core: 2. Of those that a mesh axis runs over, the one named last changes fastest.
Arguments:
- features: bfloat16 [49152, 128], P(('row', 'col')), may hold values from -6 to 6
- weight: bfloat16 [128, 256], replicated, may hold values from -0.5 to 0.5
- tile_values: bfloat16 [16, 8, 512, 128, 128], P('row', 'col'), may hold values from -0.0390625 to 0.0390625
- tile_rows: int32 [16, 8, 512], P('row', 'col'), may hold values from 0 to 23
- tile_cols: int32 [16, 8, 512], P('row', 'col'), may hold values from 0 to 47
- tile_count: int32 [16, 8], P('row', 'col'), may hold values from 1 to 512, as said below
- cotangent: bfloat16 [49152, 256], P(('row', 'col')), may hold values from -6 to 6
Outputs:
- hidden: bfloat16 [49152, 256], P(('row', 'col'))
- grad_weight: float32 [128, 256], replicated
- grad_features: bfloat16 [49152, 128], P(('row', 'col'))
The draws below stay inside these ranges and needn't reach their ends.
Inputs may be any that keep to these rules, and one draw needn't show every extreme that they name: `tile_count`: some device has all 512 slots live.
All inputs are finite; a program needn't handle non-finite values.
Results may differ from the reference program's by a relative error of at most 0.022.
Values may be sent and summed in bfloat16 or wider, within the bound.
No kernel may reach another device: no remote copies, remote signals or barrier semaphores. Data moves between devices by JAX's collectives and lax.ppermute only.
A program may use at most 128 MiB of HBM per device.

```python
import jax
import jax.numpy as jnp
from jax import lax

F_IN = 128
F_HID = 256
BS = 128
BPD = 3
TPD = 512
RB = 24
CB = 48
NODES = 49152
N_ROW = 16
N_COL = 8


def draw_tile_count(key, part):
    key = jax.random.fold_in(key, 7)
    first, second, third = jax.random.split(key, 3)
    left = jax.random.randint(first, (N_ROW * N_COL,), 0, TPD + 1)
    right = jax.random.randint(second, (N_ROW * N_COL,), 0, TPD + 1)
    counts = jnp.maximum(left * right // TPD, 1)
    chosen = jax.random.randint(third, (), 0, N_ROW * N_COL)
    counts = counts.at[chosen].set(TPD)
    return counts.reshape(N_ROW, N_COL).astype(jnp.int32)


def with_ends(array, stream_key, low, top_value):
    index_at = [jax.random.randint(jax.random.fold_in(stream_key, axis), (), 0, length) for axis, length in enumerate(array.shape)]
    longest = array.shape.index(max(array.shape))
    beside = index_at[:longest] + [(index_at[longest] + 1) % array.shape[longest]] + index_at[longest + 1:]
    return array.at[tuple(index_at)].set(low).at[tuple(beside)].set(top_value)


def levels(key, extent, pieces, least, largest):
    loudness, own = 1.0, jax.random.fold_in(key, 6)
    for position, shards_of in pieces:
        draws = jnp.exp(jax.random.uniform(jax.random.fold_in(own, position), (shards_of,), jnp.float32, least / len(pieces), largest / len(pieces)))
        loudness = loudness * jnp.repeat(draws, extent[position] // shards_of).reshape([-1 if axis == position else 1 for axis in range(len(extent))])
    return loudness


def gaussian(key, extent, deviation, most, shards=(), kind=jnp.bfloat16):
    drawn = deviation * jax.random.normal(key, extent, jnp.float32)
    if shards:
        drawn = drawn * levels(key, extent, shards, -0.22, 0.18)
    return jnp.clip(drawn, -most, most).astype(kind)


def setup_inputs(seed: int = 0) -> dict:
    splits = jax.random.split(jax.random.key(seed), 8)
    features = gaussian(splits[0], (NODES, F_IN), 1.0, 6.0, ((0, 128),))
    weight = gaussian(splits[1], (F_IN, F_HID), F_IN ** -0.5, 0.5)
    tile_values = gaussian(splits[2], (N_ROW, N_COL, TPD, BS, BS), (BS * TPD // BPD) ** -0.5, 0.0390625, ((0, 16), (1, 8)))
    tile_rows = with_ends(jax.random.randint(splits[3], (N_ROW, N_COL, TPD), 0, RB), jax.random.fold_in(splits[3], 1), 0, RB - 1).astype(jnp.int32)
    tile_cols = with_ends(jax.random.randint(splits[4], (N_ROW, N_COL, TPD), 0, CB), jax.random.fold_in(splits[4], 1), 0, CB - 1).astype(jnp.int32)
    tile_count = draw_tile_count(jax.random.fold_in(splits[7], 71), 0)
    cotangent = gaussian(splits[6], (NODES, F_HID), 1.0, 6.0, ((0, 128),))
    return dict(features=features, weight=weight, tile_values=tile_values, tile_rows=tile_rows, tile_cols=tile_cols, tile_count=tile_count, cotangent=cotangent)


def gelu_tanh(value):
    return jax.nn.gelu(value, approximate=True)

def reference(features, weight, tile_values, tile_rows, tile_cols, tile_count, cotangent):
    nblk = NODES // BS
    feat_blocks = features.reshape(nblk, BS, F_IN)
    pre_devices = jnp.arange(N_ROW * N_COL, dtype=jnp.int32)

    def locate(index):
        r_idx = index // N_COL
        c_idx = index % N_COL
        tiles = tile_values[r_idx, c_idx]
        rows = tile_rows[r_idx, c_idx]
        cols = tile_cols[r_idx, c_idx]
        live = (jnp.arange(TPD, dtype=jnp.int32) < tile_count[r_idx, c_idx]).astype(jnp.float32)
        grow = (r_idx * RB + rows).astype(jnp.int32)
        gcol = ((cols // BPD * N_COL + c_idx) * BPD + cols % BPD).astype(jnp.int32)
        return (tiles, grow, gcol, live)

    def forward_step(total, index):
        tiles, grow, gcol, live = locate(index)
        picked = feat_blocks[gcol].astype(jnp.float32)
        prod = jnp.einsum('kab,kbf->kaf', tiles.astype(jnp.float32), picked, precision=lax.Precision.HIGHEST)
        return (total.at[grow].add(prod * live[:, None, None]), None)
    total, _ = lax.scan(forward_step, jnp.zeros((nblk, BS, F_IN), jnp.float32), pre_devices)
    aggregated = total.reshape(NODES, F_IN).astype(jnp.bfloat16)
    pre = jnp.dot(aggregated, weight, preferred_element_type=jnp.float32)
    hidden = gelu_tanh(pre).astype(jnp.bfloat16)
    deriv = jax.vjp(gelu_tanh, pre)[1](cotangent.astype(jnp.float32))[0]
    delta = deriv.astype(jnp.bfloat16)
    grad_weight = jnp.dot(aggregated.T, delta, preferred_element_type=jnp.float32)
    projected = jnp.dot(delta, weight.T, preferred_element_type=jnp.float32).reshape(nblk, BS, F_IN)

    def backward_step(total, index):
        tiles, grow, gcol, live = locate(index)
        picked = projected[grow]
        prod = jnp.einsum('kba,kbf->kaf', tiles.astype(jnp.float32), picked, precision=lax.Precision.HIGHEST)
        return (total.at[gcol].add(prod * live[:, None, None]), None)
    back, _ = lax.scan(backward_step, jnp.zeros((nblk, BS, F_IN), jnp.float32), pre_devices)
    grad_features = back.reshape(NODES, F_IN).astype(jnp.bfloat16)
    return (hidden, grad_weight, grad_features)
```

```python
import jax
import jax.numpy as jnp
from jax import lax
from jax.experimental import pallas as pl
from jax.experimental.pallas import tpu as pltpu
from jax.sharding import Mesh, PartitionSpec as P

AXES = ("zl", "x", "core", "zh", "y")
ROW = ("zl", "x", "core")
COL = ("zh", "y")
BS = 128
GROUP = 4
UNROLL = 4
CHUNK = 16
MIB = 1 << 20


def schedule(key, other, live, n_keys, zero_at):
    slots = key.shape[0]
    step = GROUP * UNROLL
    places = -(-(slots + n_keys * (GROUP - 1)) // step) * step
    k = jnp.arange(slots, dtype=jnp.int32)
    keys = jnp.arange(n_keys, dtype=jnp.int32)
    here = (key[None, :] == keys[:, None]) & live[None, :]
    count = jnp.sum(here.astype(jnp.int32), axis=1)
    padded = (count + GROUP - 1) // GROUP * GROUP
    start = jnp.sum(jnp.where(keys[None, :] < keys[:, None], padded[None, :], 0), axis=1)
    own_start = jnp.sum(jnp.where(here, start[:, None], 0), axis=0)
    before = (key[:, None] == key[None, :]) & live[None, :] & (k[None, :] < k[:, None])
    place = own_start + jnp.sum(before.astype(jnp.int32), axis=1)
    place = jnp.where(live, place, -1)
    hit = place[None, :] == jnp.arange(places, dtype=jnp.int32)[:, None]
    order = jnp.sum(jnp.where(hit, k[None, :], 0), axis=1)
    source = jnp.sum(jnp.where(hit, other[None, :] - zero_at, 0), axis=1) + zero_at
    first = jnp.arange(places // GROUP, dtype=jnp.int32)[:, None] * GROUP
    inside = (start[None, :] <= first) & (first < (start + padded)[None, :])
    target = jnp.sum(jnp.where(inside, keys[None, :], 0), axis=1)
    turns = (jnp.sum(padded) + step - 1) // step
    return order, source, target, turns.reshape(1)


def load_kernel(count, tiles, held, sem):
    chunks = (count[0] + CHUNK - 1) // CHUNK

    def copy(i):
        at = pl.ds(pl.multiple_of(i * CHUNK, CHUNK), CHUNK)
        return pltpu.make_async_copy(tiles.at[at], held.at[at], sem)

    @pl.loop(0, chunks)
    def _(i):
        copy(i).start()

    @pl.loop(0, chunks)
    def _(i):
        copy(i).wait()


def load_tiles(count, tiles):
    return pl.pallas_call(
        load_kernel,
        out_shape=pltpu.VMEM(tiles.shape, tiles.dtype),
        in_specs=[
            pl.BlockSpec(memory_space=pltpu.SMEM),
            pl.BlockSpec(memory_space=pl.ANY),
        ],
        out_specs=pl.BlockSpec(memory_space=pltpu.VMEM),
        scratch_shapes=[pltpu.SemaphoreType.DMA],
        compiler_params=pltpu.CompilerParams(vmem_limit_bytes=24 * MIB),
        cost_estimate=pl.CostEstimate(
            flops=0, bytes_accessed=tiles.size * 2, transcendentals=0
        ),
        name="load_tiles",
    )(count, tiles)


def forward_kernel(order, source, target, turns, tiles, own, sib, out, feats, total):
    half = own.shape[0]
    feats[0:half] = own[...]
    feats[half : 2 * half] = sib[...]
    feats[2 * half] = jnp.zeros((BS, BS), jnp.bfloat16)
    total[...] = jnp.zeros_like(total)

    @pl.loop(0, turns[0])
    def _(turn):
        for u in range(UNROLL):
            group = turn * UNROLL + u
            at = [group * GROUP + i for i in range(GROUP)]
            left = jnp.concatenate([tiles[order[p]] for p in at], axis=1)
            right = jnp.concatenate([feats[source[p]] for p in at], axis=0)
            total[target[group]] += jnp.dot(
                left, right, preferred_element_type=jnp.float32
            )

    out[...] = total[...].astype(jnp.bfloat16)


def backward_kernel(order, source, target, turns, tiles, grads, own, sib, held, total):
    rows = grads.shape[0]
    half = own.shape[0]
    held[0:rows] = grads[...]
    held[rows] = jnp.zeros((BS, BS), jnp.bfloat16)
    total[...] = jnp.zeros_like(total)

    @pl.loop(0, turns[0])
    def _(turn):
        for u in range(UNROLL):
            group = turn * UNROLL + u
            at = [group * GROUP + i for i in range(GROUP)]
            left = jnp.concatenate([held[source[p]] for p in at], axis=1)
            right = jnp.concatenate([tiles[order[p]] for p in at], axis=0)
            total[target[group]] += jnp.dot(
                left, right, preferred_element_type=jnp.float32
            )

    own[...] = total[0:half].astype(jnp.bfloat16)
    sib[...] = total[half : 2 * half].astype(jnp.bfloat16)


def smem():
    return pl.BlockSpec(memory_space=pltpu.SMEM)


def vmem():
    return pl.BlockSpec(memory_space=pltpu.VMEM)


def forward(plan, tiles, own, sib, row_blocks):
    half = own.shape[0]
    return pl.pallas_call(
        forward_kernel,
        out_shape=jax.ShapeDtypeStruct((row_blocks, BS, BS), jnp.bfloat16),
        in_specs=[smem()] * 4 + [vmem()] * 3,
        out_specs=vmem(),
        scratch_shapes=[
            pltpu.VMEM((2 * half + 1, BS, BS), jnp.bfloat16),
            pltpu.VMEM((row_blocks, BS, BS), jnp.float32),
        ],
        compiler_params=pltpu.CompilerParams(vmem_limit_bytes=30 * MIB),
        cost_estimate=pl.CostEstimate(
            flops=2 * tiles.size * BS, bytes_accessed=tiles.size * 2, transcendentals=0
        ),
        name="forward_tiles",
    )(*plan, tiles, own, sib)


def backward(plan, tiles, grads, col_blocks):
    half = col_blocks // 2
    shape = jax.ShapeDtypeStruct((half, BS, BS), jnp.bfloat16)
    return pl.pallas_call(
        backward_kernel,
        out_shape=(shape, shape),
        in_specs=[smem()] * 4 + [vmem()] * 2,
        out_specs=(vmem(), vmem()),
        scratch_shapes=[
            pltpu.VMEM((grads.shape[0] + 1, BS, BS), jnp.bfloat16),
            pltpu.VMEM((col_blocks, BS, BS), jnp.float32),
        ],
        compiler_params=pltpu.CompilerParams(vmem_limit_bytes=30 * MIB),
        cost_estimate=pl.CostEstimate(
            flops=2 * tiles.size * BS, bytes_accessed=tiles.size * 2, transcendentals=0
        ),
        name="backward_tiles",
    )(*plan, tiles, grads)


def middle_kernel(parts, weight, cot, hidden, back, grad):
    agg = jnp.sum(parts[...].astype(jnp.float32), axis=0).astype(jnp.bfloat16)
    w = weight[...]
    pre = jnp.dot(agg, w, preferred_element_type=jnp.float32)
    scale = 0.7978845608028654
    inner = scale * (pre + 0.044715 * (pre * pre * pre))
    t = jnp.tanh(inner)
    half = 0.5 * (1.0 + t)
    hidden[...] = (pre * half).astype(jnp.bfloat16)
    slope = half + 0.5 * pre * (1.0 - t * t) * (
        scale * (1.0 + (3 * 0.044715) * (pre * pre))
    )
    delta = (cot[...].astype(jnp.float32) * slope).astype(jnp.bfloat16)
    grad[...] = lax.dot_general(
        agg, delta, (((0,), (0,)), ((), ())), preferred_element_type=jnp.float32
    ).astype(jnp.bfloat16)
    for j in range(back.shape[0]):
        back[j] = lax.dot_general(
            w,
            delta[j * BS : (j + 1) * BS],
            (((1,), (1,)), ((), ())),
            preferred_element_type=jnp.float32,
        ).astype(jnp.bfloat16)


def middle(parts, weight, cot):
    nodes = cot.shape[0]
    f_in, f_hid = weight.shape
    return pl.pallas_call(
        middle_kernel,
        out_shape=(
            jax.ShapeDtypeStruct((nodes, f_hid), jnp.bfloat16),
            jax.ShapeDtypeStruct((nodes // BS, f_in, BS), jnp.bfloat16),
            jax.ShapeDtypeStruct((f_in, f_hid), jnp.bfloat16),
        ),
        in_specs=[vmem()] * 3,
        out_specs=(vmem(),) * 3,
        compiler_params=pltpu.CompilerParams(vmem_limit_bytes=30 * MIB),
        name="middle",
    )(parts, weight, cot)


def swap_core(value):
    return lax.ppermute(value, "core", [(0, 1), (1, 0)])


def local(features, weight, tile_values, tile_rows, tile_cols, tile_count, cotangent):
    f_in, f_hid = weight.shape
    own_blocks = features.shape[0] // BS
    n_row = lax.axis_size(ROW)
    n_col = lax.axis_size(COL)
    n_half = n_row // 2
    row_blocks = own_blocks * n_col
    col_blocks = own_blocks * n_row
    tiles = tile_values[0, 0]
    count = tile_count.reshape(1)
    rows = tile_rows[0, 0]
    cols = tile_cols[0, 0]
    live = jnp.arange(tiles.shape[0], dtype=jnp.int32) < count[0]
    owner = cols // own_blocks
    side = lax.rem(owner, 2) ^ lax.axis_index("core")
    place = (side * n_half + owner // 2) * own_blocks + cols % own_blocks

    own = lax.all_to_all(
        jnp.tile(features, (n_half, 1)), ("zl", "x"), 0, 0, tiled=True
    )
    held = load_tiles(count, tiles)
    plan_f = schedule(rows, place, live, row_blocks, col_blocks)
    plan_b = schedule(place, rows, live, col_blocks, row_blocks)
    sib = swap_core(own)
    shape = (col_blocks // 2, BS, f_in)
    part = forward(plan_f, held, own.reshape(shape), sib.reshape(shape), row_blocks)
    parts = lax.all_to_all(part.reshape(row_blocks * BS, f_in), COL, 0, 0, tiled=True)
    hidden, back, grad = middle(
        parts.reshape(n_col, own_blocks * BS, f_in), weight, cotangent
    )

    lines = f_in * f_hid // (n_col * BS)
    back = back.reshape(own_blocks * BS, BS)
    send = jnp.concatenate(
        [
            jnp.broadcast_to(back[None], (n_col,) + back.shape),
            grad.reshape(n_col, lines, BS),
        ],
        axis=1,
    )
    got = lax.all_to_all(send.reshape(-1, BS), COL, 0, 0, tiled=True)
    got = got.reshape(n_col, own_blocks * BS + lines, BS)
    grads = got[:, : own_blocks * BS].reshape(row_blocks, BS, BS)
    grad_part = jnp.sum(got[:, own_blocks * BS :].astype(jnp.float32), axis=0)
    grad_part = grad_part.astype(jnp.bfloat16)

    own_sum, sib_sum = backward(plan_b, held, grads, col_blocks)
    nodes = own_blocks * BS
    sent = jnp.concatenate([sib_sum.reshape(-1, BS), grad_part], axis=0)
    other = swap_core(sent)
    pair = own_sum.reshape(-1, BS).astype(jnp.float32) + other[: -lines].astype(jnp.float32)
    grad_pair = grad_part.astype(jnp.float32) + other[-lines:].astype(jnp.float32)
    send = jnp.concatenate(
        [
            pair.astype(jnp.bfloat16).reshape(n_half, nodes, BS),
            jnp.broadcast_to(
                grad_pair.astype(jnp.bfloat16)[None], (n_half, lines, BS)
            ),
        ],
        axis=1,
    )
    got = lax.all_to_all(send.reshape(-1, BS), ("zl", "x"), 0, 0, tiled=True)
    got = jnp.sum(got.reshape(n_half, nodes + lines, BS).astype(jnp.float32), axis=0)
    grad_features = got[:nodes].astype(jnp.bfloat16).reshape(own_blocks, f_in, BS)
    grad_features = jnp.swapaxes(grad_features, 1, 2).reshape(nodes, f_in)
    grad_col = got[nodes:]
    grad_weight = lax.all_to_all(
        jnp.tile(grad_col, (n_col, 1)), COL, 0, 0, tiled=True
    ).reshape(f_in, f_hid)
    return hidden, grad_weight, grad_features


def solution(mesh):
    fine = Mesh(mesh.devices.reshape(2, 4, 2, 2, 4), AXES)
    nodes = P(AXES, None)
    mapped = jax.shard_map(
        local,
        mesh=fine,
        in_specs=(
            nodes,
            P(),
            P(ROW, COL, None, None, None),
            P(ROW, COL, None),
            P(ROW, COL, None),
            P(ROW, COL),
            nodes,
        ),
        out_specs=(nodes, P(), nodes),
        check_vma=False,
    )
    return mapped
```

```python
import functools

import jax
import jax.numpy as jnp
from jax import lax
from jax.experimental import pallas as pl
from jax.experimental.pallas import tpu as pltpu
from jax.sharding import Mesh, PartitionSpec as P

AXES = ("zl", "x", "core", "zh", "y")
ROW = ("zl", "x", "core")
COL = ("zh", "y")
BS = 128
GROUP = 4
UNROLL = 16
CHUNK = 16
LIMIT = 24 << 20


def make_plan(key, other, live, n_keys, zero_at, places, plan):
    slots = key.shape[1]
    keys = lax.broadcasted_iota(jnp.int32, (n_keys, slots), 0)
    here = (keys == key) & live
    marks = jnp.where(here, 1.0, 0.0)
    earlier = lax.broadcasted_iota(jnp.int32, (slots, slots), 0)
    earlier = earlier < lax.broadcasted_iota(jnp.int32, (slots, slots), 1)
    rank = jnp.dot(
        marks.astype(jnp.bfloat16),
        jnp.where(earlier, 1.0, 0.0).astype(jnp.bfloat16),
        preferred_element_type=jnp.float32,
    )
    count = jnp.sum(marks, axis=1, keepdims=True).astype(jnp.int32)
    groups = lax.div(count + (GROUP - 1), GROUP)
    lower = lax.broadcasted_iota(jnp.int32, (n_keys, n_keys), 1)
    lower = lower < lax.broadcasted_iota(jnp.int32, (n_keys, n_keys), 0)
    start = jnp.dot(
        jnp.where(lower, 1.0, 0.0).astype(jnp.bfloat16),
        jnp.broadcast_to(groups, (n_keys, 128)).astype(jnp.bfloat16),
        preferred_element_type=jnp.float32,
    )[:, :1].astype(jnp.int32)
    place = jnp.where(here, rank.astype(jnp.int32) + start * GROUP, 0)
    place = jnp.where(live, jnp.sum(place, axis=0, keepdims=True), -1)
    hit = lax.broadcasted_iota(jnp.int32, (places, slots), 0) == place
    hit = jnp.where(hit, 1.0, 0.0).astype(jnp.bfloat16)
    k = lax.broadcasted_iota(jnp.int32, (8, slots), 1)
    row = lax.broadcasted_iota(jnp.int32, (8, slots), 0)
    values = jnp.where(
        row == 0, k & 255, jnp.where(row == 1, k - (k & 255), jnp.where(row == 2, other - zero_at, 0))
    )
    values = values.astype(jnp.float32).astype(jnp.bfloat16)
    found = lax.dot_general(
        values, hit, (((1,), (1,)), ((), ())), preferred_element_type=jnp.float32
    ).astype(jnp.int32)
    group = lax.broadcasted_iota(jnp.int32, (n_keys, places), 1)
    inside = (start <= group) & (group < start + groups)
    names = lax.broadcasted_iota(jnp.int32, (n_keys, places), 0)
    target = jnp.sum(jnp.where(inside, names, 0), axis=0, keepdims=True)
    turns = lax.div(jnp.sum(groups, axis=0, keepdims=True) + (UNROLL - 1), UNROLL)
    plan[0:1] = found[0:1] + found[1:2]
    plan[1:2] = found[2:3] + zero_at
    plan[2:3] = target
    plan[3:4] = jnp.broadcast_to(turns, (1, places))


def places_of(slots, n_keys):
    step = max(GROUP * UNROLL, 128)
    return -(-(slots + n_keys * (GROUP - 1)) // step) * step


def load_kernel(n_row_blocks, n_col_blocks, count, tiles, rows, place, dest, held, plan_f, plan_b, sem):
    chunks = (count[0, 0] + CHUNK - 1) // CHUNK

    def copy(i):
        at = pl.ds(pl.multiple_of(i * CHUNK, CHUNK), CHUNK)
        return pltpu.make_async_copy(tiles.at[at], held.at[at], sem)

    @pl.loop(0, chunks)
    def _(i):
        copy(i).start()

    live = lax.broadcasted_iota(jnp.int32, rows.shape, 1) < count[0, 0]
    make_plan(rows[...], place[...], live, n_row_blocks, n_col_blocks, plan_f.shape[1], plan_f)
    make_plan(dest[...], rows[...], live, n_col_blocks, n_row_blocks, plan_b.shape[1], plan_b)

    @pl.loop(0, chunks)
    def _(i):
        copy(i).wait()


def load_tiles(count, tiles, rows, place, dest, n_row_blocks, n_col_blocks):
    slots = tiles.shape[0]
    return pl.pallas_call(
        functools.partial(load_kernel, n_row_blocks, n_col_blocks),
        out_shape=(
            pltpu.VMEM(tiles.shape, tiles.dtype),
            jax.ShapeDtypeStruct((4, places_of(slots, n_row_blocks)), jnp.int32),
            jax.ShapeDtypeStruct((4, places_of(slots, n_col_blocks)), jnp.int32),
        ),
        in_specs=[smem(), pl.BlockSpec(memory_space=pltpu.HBM)] + [vmem()] * 3,
        out_specs=(vmem(),) * 3,
        scratch_shapes=[pltpu.SemaphoreType.DMA],
        compiler_params=pltpu.CompilerParams(vmem_limit_bytes=LIMIT),
        cost_estimate=pl.CostEstimate(
            flops=0, bytes_accessed=tiles.size * 2, transcendentals=0
        ),
        name="load_tiles",
    )(count, tiles, rows, place, dest)


def forward_kernel(plan, tiles, *refs):
    blocks, (out, feats, total) = refs[:-3], refs[-3:]
    each = blocks[0].shape[0]
    for n, block in enumerate(blocks):
        feats[n * each : (n + 1) * each] = block[...]
    feats[len(blocks) * each] = jnp.zeros((BS, BS), jnp.bfloat16)
    total[...] = jnp.zeros_like(total)

    @pl.loop(0, plan[3, 0])
    def _(turn):
        for u in range(UNROLL):
            group = turn * UNROLL + u
            at = [group * GROUP + i for i in range(GROUP)]
            left = jnp.concatenate([tiles[plan[0, p]] for p in at], axis=1)
            right = jnp.concatenate([feats[plan[1, p]] for p in at], axis=0)
            total[plan[2, group]] += jnp.dot(
                left, right, preferred_element_type=jnp.float32
            )

    out[...] = total[...].astype(jnp.bfloat16)


def backward_kernel(plan, tiles, got, own, sib, grad_sum, held, total):
    n_col, lines, _ = got.shape
    half = own.shape[0]
    each = held.shape[0] // n_col
    for n in range(n_col):
        for j in range(each):
            held[n * each + j] = got[n, j * BS : (j + 1) * BS]
    held[n_col * each] = jnp.zeros((BS, BS), jnp.bfloat16)
    total[...] = jnp.zeros_like(total)
    grad_lines = got[:, each * BS : lines].astype(jnp.float32)
    grad_sum[...] = jnp.sum(grad_lines, axis=0).astype(jnp.bfloat16)

    @pl.loop(0, plan[3, 0])
    def _(turn):
        for u in range(UNROLL):
            group = turn * UNROLL + u
            at = [group * GROUP + i for i in range(GROUP)]
            left = jnp.concatenate([held[plan[1, p]] for p in at], axis=1)
            right = jnp.concatenate([tiles[plan[0, p]] for p in at], axis=0)
            total[plan[2, group]] += jnp.dot(
                left, right, preferred_element_type=jnp.float32
            )

    own[...] = total[0:half].astype(jnp.bfloat16)
    sib[...] = total[half : 2 * half].astype(jnp.bfloat16)


def smem():
    return pl.BlockSpec(memory_space=pltpu.SMEM)


def vmem():
    return pl.BlockSpec(memory_space=pltpu.VMEM)


def tile_cost(tiles):
    return pl.CostEstimate(
        flops=2 * tiles.size * BS, bytes_accessed=tiles.size * 2, transcendentals=0
    )


def forward(plan, tiles, blocks, row_blocks):
    col_blocks = sum(b.shape[0] for b in blocks)
    return pl.pallas_call(
        forward_kernel,
        out_shape=jax.ShapeDtypeStruct((row_blocks, BS, BS), jnp.bfloat16),
        in_specs=[smem()] + [vmem()] * (1 + len(blocks)),
        out_specs=vmem(),
        scratch_shapes=[
            pltpu.VMEM((col_blocks + 1, BS, BS), jnp.bfloat16),
            pltpu.VMEM((row_blocks, BS, BS), jnp.float32),
        ],
        compiler_params=pltpu.CompilerParams(vmem_limit_bytes=LIMIT),
        cost_estimate=tile_cost(tiles),
        name="forward_tiles",
    )(plan, tiles, *blocks)


def backward(plan, tiles, got, own_blocks, col_blocks):
    half = col_blocks // 2
    n_col, lines, _ = got.shape
    row_blocks = n_col * own_blocks
    shape = jax.ShapeDtypeStruct((half, BS, BS), jnp.bfloat16)
    grad_lines = lines - own_blocks * BS
    return pl.pallas_call(
        backward_kernel,
        out_shape=(shape, shape, jax.ShapeDtypeStruct((grad_lines, BS), jnp.bfloat16)),
        in_specs=[smem()] + [vmem()] * 2,
        out_specs=(vmem(),) * 3,
        scratch_shapes=[
            pltpu.VMEM((row_blocks + 1, BS, BS), jnp.bfloat16),
            pltpu.VMEM((col_blocks, BS, BS), jnp.float32),
        ],
        compiler_params=pltpu.CompilerParams(vmem_limit_bytes=LIMIT),
        cost_estimate=tile_cost(tiles),
        name="backward_tiles",
    )(plan, tiles, got)


def middle_kernel(parts, weight, cot, hidden, send):
    agg = jnp.sum(parts[...].astype(jnp.float32), axis=0).astype(jnp.bfloat16)
    w = weight[...]
    pre = jnp.dot(agg, w, preferred_element_type=jnp.float32)
    scale = 0.7978845608028654
    inner = scale * (pre + 0.044715 * (pre * pre * pre))
    t = jnp.tanh(inner)
    half = 0.5 * (1.0 + t)
    hidden[...] = (pre * half).astype(jnp.bfloat16)
    slope = half + 0.5 * pre * (1.0 - t * t) * (
        scale * (1.0 + (3 * 0.044715) * (pre * pre))
    )
    delta = (cot[...].astype(jnp.float32) * slope).astype(jnp.bfloat16)
    grad = lax.dot_general(
        agg, delta, (((0,), (0,)), ((), ())), preferred_element_type=jnp.float32
    ).astype(jnp.bfloat16)
    n_col, nodes = send.shape[0], agg.shape[0]
    for j in range(nodes // BS):
        back = lax.dot_general(
            w,
            delta[j * BS : (j + 1) * BS],
            (((1,), (1,)), ((), ())),
            preferred_element_type=jnp.float32,
        ).astype(jnp.bfloat16)
        for n in range(n_col):
            send[n, j * BS : (j + 1) * BS] = back
    rows = grad.shape[0]
    for i in range(grad.shape[1] // BS):
        for n in range(n_col):
            send[n, nodes + i * rows : nodes + (i + 1) * rows] = grad[:, i * BS : (i + 1) * BS]


def middle(parts, weight, cot):
    nodes = cot.shape[0]
    f_in, f_hid = weight.shape
    lines = nodes + f_in * f_hid // BS
    return pl.pallas_call(
        middle_kernel,
        out_shape=(
            jax.ShapeDtypeStruct((nodes, f_hid), jnp.bfloat16),
            jax.ShapeDtypeStruct((parts.shape[0], lines, BS), jnp.bfloat16),
        ),
        in_specs=[vmem()] * 3,
        out_specs=(vmem(),) * 2,
        compiler_params=pltpu.CompilerParams(vmem_limit_bytes=LIMIT),
        name="middle",
    )(parts, weight, cot)


def pair_kernel(own, sib, grad, other_grad, send):
    n_half, lines, _ = send.shape
    each = own.shape[0] // n_half
    both = grad[...].astype(jnp.float32) + other_grad[...].astype(jnp.float32)
    both = both.astype(jnp.bfloat16)
    for n in range(n_half):
        for j in range(each):
            at = n * each + j
            total = own[at].astype(jnp.float32) + sib[at].astype(jnp.float32)
            send[n, j * BS : (j + 1) * BS] = total.astype(jnp.bfloat16)
        send[n, each * BS : lines] = both


def pair(own, sib, grad, other_grad, n_half):
    lines = own.shape[0] // n_half * BS + grad.shape[0]
    return pl.pallas_call(
        pair_kernel,
        out_shape=jax.ShapeDtypeStruct((n_half, lines, BS), jnp.bfloat16),
        in_specs=[vmem()] * 4,
        out_specs=vmem(),
        compiler_params=pltpu.CompilerParams(vmem_limit_bytes=LIMIT),
        name="pair",
    )(own, sib, grad, other_grad)


def last_kernel(got, grad_features, grad_weight):
    nodes = grad_features.shape[0]
    total = jnp.sum(got[...].astype(jnp.float32), axis=0)
    for j in range(nodes // BS):
        at = slice(j * BS, (j + 1) * BS)
        grad_features[at] = total[at].T.astype(jnp.bfloat16)
    rows = grad_weight.shape[0]
    for i in range(grad_weight.shape[1] // BS):
        at = slice(nodes + i * rows, nodes + (i + 1) * rows)
        grad_weight[:, i * BS : (i + 1) * BS] = total[at]


def last(got, nodes, f_in, f_hid):
    return pl.pallas_call(
        last_kernel,
        out_shape=(
            jax.ShapeDtypeStruct((nodes, f_in), jnp.bfloat16),
            jax.ShapeDtypeStruct((f_in, f_hid), jnp.float32),
        ),
        in_specs=[vmem()],
        out_specs=(vmem(),) * 2,
        compiler_params=pltpu.CompilerParams(vmem_limit_bytes=LIMIT),
        name="last",
    )(got)


def swap_core(value):
    return lax.ppermute(value, "core", [(0, 1), (1, 0)])


def shift(value, axis, by):
    n = lax.axis_size(axis)
    return lax.ppermute(value, axis, [(i, (i + by) % n) for i in range(n)])


def local(features, weight, tile_values, tile_rows, tile_cols, tile_count, cotangent):
    f_in, f_hid = weight.shape
    nodes = features.shape[0]
    own_blocks = nodes // BS
    n_x, n_zl = lax.axis_size("x"), lax.axis_size("zl")
    n_col = lax.axis_size(COL)
    n_half = n_x * n_zl
    row_blocks = own_blocks * n_col
    col_blocks = own_blocks * n_half * 2
    tiles = tile_values[0, 0]
    rows = tile_rows[0]
    cols = tile_cols[0]
    owner = cols // own_blocks
    inner = cols - owner * own_blocks
    side = (owner & 1) ^ lax.axis_index("core")
    owner = owner >> 1
    turned = ((owner // n_x) ^ lax.axis_index("zl")) * n_x + (
        (lax.axis_index("x") - owner) & (n_x - 1)
    )
    place = (side * n_half + turned) * own_blocks + inner
    dest = (side * n_half + owner) * own_blocks + inner

    near = [features] + [shift(features, "x", by) for by in range(1, n_x)]
    far = [shift(features, "zl", 1)]
    held, plan_f, plan_b = load_tiles(
        tile_count, tiles, rows, place, dest, row_blocks, col_blocks
    )
    near, far, held = lax.optimization_barrier((near, far, held))
    far += [shift(near[1], "zl", 1), shift(far[0], "x", 2), shift(near[3], "zl", 1)]
    mine = near + far
    other = [swap_core(block) for block in mine]
    blocks = [b.reshape(own_blocks, BS, f_in) for b in mine + other]
    part = forward(plan_f, held, blocks, row_blocks)
    parts = lax.all_to_all(part.reshape(row_blocks * BS, f_in), COL, 0, 0, tiled=True)
    hidden, send = middle(parts.reshape(n_col, nodes, f_in), weight, cotangent)

    got = lax.all_to_all(send.reshape(-1, BS), COL, 0, 0, tiled=True)
    own, sib, grad = backward(
        plan_b, held, got.reshape(send.shape), own_blocks, col_blocks
    )
    send = pair(own, swap_core(sib), grad, swap_core(grad), n_half)
    got = lax.all_to_all(send.reshape(-1, BS), ("zl", "x"), 0, 0, tiled=True)
    grad_features, grad_weight = last(got.reshape(send.shape), nodes, f_in, f_hid)
    return hidden, grad_weight, grad_features


def solution(mesh):
    fine = Mesh(mesh.devices.reshape(2, 4, 2, 2, 4), AXES)
    nodes = P(AXES, None)
    mapped = jax.shard_map(
        local,
        mesh=fine,
        in_specs=(
            nodes,
            P(),
            P(ROW, COL, None, None, None),
            P(ROW, COL, None),
            P(ROW, COL, None),
            P(ROW, COL),
            nodes,
        ),
        out_specs=(nodes, P(), nodes),
        check_vma=False,
    )
    return mapped
```

```python
import functools

import jax
import jax.numpy as jnp
from jax import lax
from jax.experimental import pallas as pl
from jax.experimental.pallas import tpu as pltpu
from jax.sharding import Mesh, PartitionSpec as P

AXES = ("zl", "x", "core", "zh", "y")
ROW = ("zl", "x", "core")
COL = ("zh", "y")
BS = 128
SHIFT = 10
FORWARD = (2, 32)
BACKWARD = (2, 32)
LIMIT = 24 << 20
CHUNK = 16
SMALL = pl.CostEstimate(flops=BS, bytes_accessed=BS, transcendentals=0)


def smem():
    return pl.BlockSpec(memory_space=pltpu.SMEM)


def vmem():
    return pl.BlockSpec(memory_space=pltpu.VMEM)


def hbm():
    return pl.BlockSpec(memory_space=pltpu.HBM)


def iota(shape, dim):
    return lax.broadcasted_iota(jnp.int32, shape, dim)


def places_of(slots, bounds, form):
    group, unroll = form
    groups = (slots + bounds[-1] * (group - 1)) // group
    groups += (len(bounds) - 1) * (unroll - 1)
    return -(-groups // 128) * 128 * group


def plan_size(places, form):
    return places + places // form[0] + 128


def places_in(plan, form):
    group, _ = form
    return (plan.shape[1] - 128) // (group + 1) * group


def make_plan(key, bounds, other, live, form, plan):
    group, unroll = form
    n_keys = bounds[-1]
    slots = key.shape[1]
    places = places_in(plan, form)
    targets = places // group
    here = (iota((n_keys, slots), 0) == key) & live
    marks = jnp.where(here, 1.0, 0.0)
    earlier = iota((slots, slots), 0) < iota((slots, slots), 1)
    rank = jnp.dot(
        marks.astype(jnp.bfloat16),
        jnp.where(earlier, 1.0, 0.0).astype(jnp.bfloat16),
        preferred_element_type=jnp.float32,
    )
    count = jnp.sum(marks, axis=1, keepdims=True).astype(jnp.int32)
    groups = lax.div(count + (group - 1), group)
    lower = iota((n_keys, n_keys), 1) < iota((n_keys, n_keys), 0)
    start = jnp.dot(
        jnp.where(lower, 1.0, 0.0).astype(jnp.bfloat16),
        jnp.broadcast_to(groups, (n_keys, 128)).astype(jnp.bfloat16),
        preferred_element_type=jnp.float32,
    )[:, :1].astype(jnp.int32)
    name = iota((n_keys, 1), 0)
    done = turns = jnp.zeros((1, 1), jnp.int32)
    ends = []
    for lo, hi in zip(bounds, bounds[1:]):
        inside = (name >= lo) & (name < hi)
        start = start + jnp.where(inside, turns * unroll - done, 0)
        here_now = jnp.sum(jnp.where(inside, groups, 0), axis=0, keepdims=True)
        done = done + here_now
        turns = turns + lax.div(here_now + (unroll - 1), unroll)
        ends.append(turns)
    place = jnp.where(here, rank.astype(jnp.int32) + start * group, 0)
    place = jnp.where(live, jnp.sum(place, axis=0, keepdims=True), -1)
    hit = iota((places, slots), 0) == place
    hit = jnp.where(hit, 1.0, 0.0).astype(jnp.bfloat16)
    row = iota((8, slots), 0)
    ids = iota((8, slots), 1) - slots
    low = ids & 127
    values = jnp.where(row == 1, ids - low, jnp.where(row == 2, other, 0))
    values = jnp.where(row == 0, low, values)
    found = lax.dot_general(
        values.astype(jnp.float32).astype(jnp.bfloat16),
        hit,
        (((1,), (1,)), ((), ())),
        preferred_element_type=jnp.float32,
    ).astype(jnp.int32)
    at = iota((n_keys, targets), 1)
    inside = (start <= at) & (at < start + groups)
    names = iota((n_keys, targets), 0)
    base = jnp.zeros_like(names)
    for lo in bounds[1:-1]:
        base = jnp.where(names >= lo, lo, base)
    names = names - base
    tile = found[0:1] + found[1:2] + slots
    plan[0:1, 0:places] = tile + (found[2:3] << SHIFT)
    plan[0:1, places : places + targets] = jnp.sum(
        jnp.where(inside, names, 0), axis=0, keepdims=True
    )
    lane = iota((1, 128), 1)
    last = jnp.zeros((1, 128), jnp.int32)
    for n, end in enumerate(ends):
        last = jnp.where(lane == n + 1, end, last)
    plan[0:1, places + targets :] = last


def divided(value, by, most):
    return sum(jnp.where(value >= by * t, 1, 0) for t in range(1, most // by + 1))


def plan_kernel(
    sizes, where, count, rows, cols, tiles, plan_f, plan_b, held, row_in, col_in, sem
):
    lo, hi = chunks_of(count, tiles, 0)

    copies = [
        pltpu.make_async_copy(rows, row_in, sem.at[0]),
        pltpu.make_async_copy(cols, col_in, sem.at[1]),
    ]
    for copy in copies:
        copy.start()

    @pl.loop(lo, hi)
    def _(i):
        chunk_copy(tiles, held, sem.at[2], i).start()

    held[tiles.shape[0]] = jnp.zeros((BS, BS), jnp.bfloat16)
    for copy in copies:
        copy.wait()
    own_blocks, row_blocks, col_blocks = sizes
    core, x, zl, y, zh = [where[i] for i in range(5)]
    row, col = row_in[...], col_in[...]
    live = iota(row.shape, 1) < count[0, 0]
    owner = divided(col, own_blocks, col_blocks - 1)
    inner = col - owner * own_blocks
    side = (owner & 1) ^ core
    half = col_blocks // 2
    owner = owner >> 1
    turned = ((owner >> 2) ^ zl) * 4 + ((x - (owner & 3)) & 3)
    spot = side * half + turned * own_blocks + inner
    dest = (1 - side) * half + owner * own_blocks + inner

    owner = divided(row, own_blocks, row_blocks - 1)
    inner = row - owner * own_blocks
    inner = inner + ((owner >> 2) ^ zh) * own_blocks
    each = row_blocks // 4
    later = jnp.where(iota(row.shape, 1) >= row.shape[1] // 2, 2, 0)
    ahead = ((owner & 3) - y) & 3
    turn = jnp.where(ahead == 2, later, jnp.where(ahead == 1, later + 1, 4))
    key = jnp.where(ahead == 0, 5, turn) * each + inner
    make_plan(key, forward_bounds(sizes), spot, live, FORWARD, plan_f)
    behind = (y - (owner & 3)) & 3
    spot = (behind & 1) * each + inner
    key = dest + jnp.where(behind >= 2, col_blocks, 0)
    make_plan(key, backward_bounds(sizes), spot, live, BACKWARD, plan_b)

    @pl.loop(lo, hi)
    def _(i):
        chunk_copy(tiles, held, sem.at[2], i).wait()


def forward_bounds(sizes):
    each = sizes[1] // 4
    return (0, 2 * each, 4 * each, 5 * each, 6 * each)


def backward_bounds(sizes):
    columns = sizes[2]
    return (0, columns, columns + columns // 2, 2 * columns)


def make_plans(sizes, where, count, rows, cols, tiles):
    slots = rows.shape[1]
    places_f = places_of(slots, forward_bounds(sizes), FORWARD)
    places_b = places_of(slots, backward_bounds(sizes), BACKWARD)
    return pl.pallas_call(
        functools.partial(plan_kernel, sizes),
        out_shape=(
            jax.ShapeDtypeStruct((1, plan_size(places_f, FORWARD)), jnp.int32),
            jax.ShapeDtypeStruct((1, plan_size(places_b, BACKWARD)), jnp.int32),
            pltpu.VMEM((tiles.shape[0] + 1, BS, BS), tiles.dtype),
        ),
        in_specs=[smem()] * 2 + [hbm()] * 3,
        out_specs=(vmem(),) * 3,
        scratch_shapes=[pltpu.VMEM(rows.shape, jnp.int32)] * 2
        + [pltpu.SemaphoreType.DMA((3,))],
        compiler_params=pltpu.CompilerParams(vmem_limit_bytes=LIMIT),
        cost_estimate=pl.CostEstimate(
            flops=0, bytes_accessed=tiles.size, transcendentals=0
        ),
        name="make_plans",
    )(where, count, rows, cols, tiles)


def chunks_of(count, tiles, part):
    most = tiles.shape[0] // CHUNK // 2
    live = lax.div(count[0, 0] + (CHUNK - 1), CHUNK)
    return part * most, jnp.minimum(live, (part + 1) * most)


def chunk_copy(tiles, held, sem, i):
    at = pl.ds(pl.multiple_of(i * CHUNK, CHUNK), CHUNK)
    return pltpu.make_async_copy(tiles.at[at], held.at[at], sem)


def multiply(plan, phases, form, tiles, source, tile_first, total):
    group, unroll = form
    places = places_in(plan, form)
    targets = places // group
    lo, hi = [plan[0, places + targets + phase] for phase in phases]

    @pl.loop(lo, hi)
    def _(turn):
        for u in range(unroll):
            at = turn * unroll + u
            spots = [plan[0, at * group + i] for i in range(group)]
            left = [tiles[spot & ((1 << SHIFT) - 1)] for spot in spots]
            right = [source[spot >> SHIFT] for spot in spots]
            if not tile_first:
                left, right = right, left
            total[plan[0, places + at]] += jnp.dot(
                jnp.concatenate(left, axis=1),
                jnp.concatenate(right, axis=0),
                preferred_element_type=jnp.float32,
            )


def forward_first_kernel(plan, count, tiles, _, *refs):
    blocks, (out, after, held, feats, total, sem) = refs[:-6], refs[-6:]
    lo, hi = chunks_of(count, tiles, 1)

    @pl.loop(lo, hi)
    def _(i):
        chunk_copy(tiles, held, sem, i).start()

    each = blocks[0].shape[0]
    for n, block in enumerate(blocks):
        feats[n * each : (n + 1) * each] = block[...]
    total[...] = jnp.zeros_like(total)

    multiply(plan, (0, 1), FORWARD, held, feats, True, total)

    @pl.loop(lo, hi)
    def _(i):
        chunk_copy(tiles, held, sem, i).wait()

    multiply(plan, (1, 2), FORWARD, held, feats, True, total)
    half = out.shape[0]
    out[...] = total[0:half].astype(jnp.bfloat16)
    after[...] = total[half : 2 * half].astype(jnp.bfloat16)


def forward_next_kernel(phase, plan, held, feats, out, *scratch):
    total = scratch[0] if scratch else out
    total[...] = jnp.zeros_like(total)
    multiply(plan, (phase, phase + 1), FORWARD, held, feats, True, total)
    if scratch:
        out[...] = total[...].astype(jnp.bfloat16)


def put_sources(source, first, second):
    each = source.shape[0] // 2
    source[0:each] = first[0:each]
    source[each : 2 * each] = second[0:each]


def backward_near_kernel(plan, held, first, second, total, source):
    put_sources(source, first, second)
    total[...] = jnp.zeros_like(total)
    multiply(plan, (0, 1), BACKWARD, held, source, False, total)


def backward_sib_kernel(plan, held, first, second, before, near, next_, out, both, source, total):
    put_sources(source, first, second)
    each = source.shape[0] // 2
    parts = [block[each:].astype(jnp.float32) for block in (near, next_, first, second)]
    both[...] = sum(parts).astype(jnp.bfloat16)
    total[...] = before[0 : total.shape[0]]
    multiply(plan, (1, 2), BACKWARD, held, source, False, total)
    out[...] = total[...].astype(jnp.bfloat16)


def backward_own_kernel(plan, held, first, second, before, out, source, total):
    put_sources(source, first, second)
    half = total.shape[0]
    total[...] = before[half : 2 * half]
    multiply(plan, (2, 3), BACKWARD, held, source, False, total)
    out[...] = total[...].astype(jnp.bfloat16)


def add_kernel(total, first, second, third, keep, send):
    parts = [part[...].astype(jnp.float32) for part in (first, second, third)]
    total = total[...] + sum(parts)
    each = keep.shape[0]
    keep[...] = total[0:each]
    send[...] = total[each : 2 * each].astype(jnp.bfloat16)


def collect_kernel(own, other, send):
    each = send.shape[0] - own.shape[0]
    send[0:each] = own[0:each]
    send[each : 2 * each] = other[0:each]
    grad = own[each:].astype(jnp.float32) + other[each:].astype(jnp.float32)
    send[2 * each :] = grad.astype(jnp.bfloat16)


def kernel_call(kernel, name, outs, n_smem, *args, scratch=(), aliases={}, in_hbm=()):
    specs = [smem() if n < n_smem else vmem() for n in range(len(args))]
    specs = [hbm() if n in in_hbm else spec for n, spec in enumerate(specs)]
    return pl.pallas_call(
        kernel,
        out_shape=tuple(outs),
        in_specs=specs,
        out_specs=(vmem(),) * len(outs),
        scratch_shapes=list(scratch),
        input_output_aliases=aliases,
        compiler_params=pltpu.CompilerParams(vmem_limit_bytes=LIMIT),
        cost_estimate=SMALL,
        name=name,
    )(*args)


def of_blocks(n, dtype=jnp.bfloat16):
    return jax.ShapeDtypeStruct((n, BS, BS), dtype)


def sums(n):
    return pltpu.VMEM((n, BS, BS), jnp.float32)


def middle_kernel(weight, cot, *refs):
    parts, (hidden, send) = refs[:-2], refs[-2:]
    agg = sum(part[...].astype(jnp.float32) for part in parts).astype(jnp.bfloat16)
    w = weight[...]
    pre = jnp.dot(agg, w, preferred_element_type=jnp.float32)
    scale = 0.7978845608028654
    inner = scale * (pre + 0.044715 * (pre * pre * pre))
    t = jnp.tanh(inner)
    half = 0.5 * (1.0 + t)
    hidden[...] = (pre * half).astype(jnp.bfloat16)
    slope = half + 0.5 * pre * (1.0 - t * t) * (
        scale * (1.0 + (3 * 0.044715) * (pre * pre))
    )
    delta = (cot[...].astype(jnp.float32) * slope).astype(jnp.bfloat16)
    grad = lax.dot_general(
        agg, delta, (((0,), (0,)), ((), ())), preferred_element_type=jnp.float32
    ).astype(jnp.bfloat16)
    each = agg.shape[0] // BS
    for j in range(each):
        send[j] = lax.dot_general(
            w,
            delta[j * BS : (j + 1) * BS],
            (((1,), (1,)), ((), ())),
            preferred_element_type=jnp.float32,
        ).astype(jnp.bfloat16)
    for i in range(grad.shape[1] // BS):
        send[each + i] = grad[:, i * BS : (i + 1) * BS]


def pair_kernel(own, sib, grad, other_grad, send):
    n_half, lines, _ = send.shape
    each = own.shape[0] // n_half
    both = grad[...].astype(jnp.float32) + other_grad[...].astype(jnp.float32)
    both = both.astype(jnp.bfloat16).reshape(-1, BS)
    for n in range(n_half):
        for j in range(each):
            at = n * each + j
            total = own[at].astype(jnp.float32) + sib[at].astype(jnp.float32)
            send[n, j * BS : (j + 1) * BS] = total.astype(jnp.bfloat16)
        send[n, each * BS : lines] = both


def pair(own, sib, grad, other_grad, n_half):
    lines = (own.shape[0] // n_half + grad.shape[0]) * BS
    return pl.pallas_call(
        pair_kernel,
        out_shape=jax.ShapeDtypeStruct((n_half, lines, BS), jnp.bfloat16),
        in_specs=[vmem()] * 4,
        out_specs=vmem(),
        compiler_params=pltpu.CompilerParams(vmem_limit_bytes=LIMIT),
        name="pair",
    )(own, sib, grad, other_grad)


def last_kernel(got, grad_features, grad_weight):
    nodes = grad_features.shape[0]
    total = jnp.sum(got[...].astype(jnp.float32), axis=0)
    for j in range(nodes // BS):
        at = slice(j * BS, (j + 1) * BS)
        grad_features[at] = total[at].T.astype(jnp.bfloat16)
    rows = grad_weight.shape[0]
    for i in range(grad_weight.shape[1] // BS):
        at = slice(nodes + i * rows, nodes + (i + 1) * rows)
        grad_weight[:, i * BS : (i + 1) * BS] = total[at]


def last(got, nodes, f_in, f_hid):
    return pl.pallas_call(
        last_kernel,
        out_shape=(
            jax.ShapeDtypeStruct((nodes, f_in), jnp.bfloat16),
            jax.ShapeDtypeStruct((f_in, f_hid), jnp.float32),
        ),
        in_specs=[vmem()],
        out_specs=(vmem(),) * 2,
        compiler_params=pltpu.CompilerParams(vmem_limit_bytes=LIMIT),
        name="last",
    )(got)


def swap_core(value):
    return lax.ppermute(value, "core", [(0, 1), (1, 0)])


def shift(value, axis, by):
    n = lax.axis_size(axis)
    return lax.ppermute(value, axis, [(i, (i + by) % n) for i in range(n)])


def local(features, weight, tile_values, tile_rows, tile_cols, tile_count, cotangent):
    f_in, f_hid = weight.shape
    nodes = features.shape[0]
    own_blocks = nodes // BS
    n_x, n_zl = lax.axis_size("x"), lax.axis_size("zl")
    n_col = lax.axis_size(COL)
    n_half = n_x * n_zl
    row_blocks = own_blocks * n_col
    col_blocks = own_blocks * n_half * 2
    tiles = pltpu.with_memory_space_constraint(tile_values[0, 0], pltpu.HBM)
    sent_blocks = own_blocks + f_in * f_hid // (BS * BS)
    sizes = (own_blocks, row_blocks, col_blocks)
    rows = pltpu.with_memory_space_constraint(tile_rows[0], pltpu.HBM)
    cols = pltpu.with_memory_space_constraint(tile_cols[0], pltpu.HBM)
    where = jnp.stack([lax.axis_index(a) for a in ("core", "x", "zl", "y", "zh")])

    near = [features] + [shift(features, "x", by) for by in range(1, n_x)]
    far = [shift(features, "zl", 1)]
    plan_f, plan_b, held = make_plans(sizes, where, tile_count, rows, cols, tiles)
    near, far, held = lax.optimization_barrier((near, far, held))
    far += [shift(near[1], "zl", 1), shift(far[0], "x", 2), shift(near[3], "zl", 1)]
    other = [swap_core(block) for block in near + far]
    blocks = [b.reshape(own_blocks, BS, f_in) for b in near + far + other]

    each = row_blocks // 4
    first, second, held, feats = kernel_call(
        forward_first_kernel,
        "forward_first",
        [
            of_blocks(each),
            of_blocks(each),
            pltpu.VMEM(held.shape, held.dtype),
            of_blocks(col_blocks),
        ],
        2,
        plan_f,
        tile_count,
        tiles,
        held,
        *blocks,
        scratch=[sums(2 * each), pltpu.SemaphoreType.DMA],
        aliases={3: 2},
        in_hbm=(2,),
    )
    got = [shift(first, "y", 2), shift(second, "y", 1)]
    (third,) = kernel_call(
        functools.partial(forward_next_kernel, 2),
        "forward_next",
        [of_blocks(each)],
        1,
        plan_f,
        held,
        feats,
        scratch=[sums(each)],
    )
    got.append(shift(third, "y", 3))
    held, feats, third = lax.optimization_barrier((held, feats, third))
    (total,) = kernel_call(
        functools.partial(forward_next_kernel, 3),
        "forward_here",
        [of_blocks(each, jnp.float32)],
        1,
        plan_f,
        held,
        feats,
    )
    keep, send = kernel_call(
        add_kernel,
        "add",
        [of_blocks(own_blocks, jnp.float32), of_blocks(own_blocks)],
        0,
        total,
        *got,
    )
    parts = [part.reshape(nodes, f_in) for part in (keep, shift(send, "zh", 1))]
    hidden, send = kernel_call(
        middle_kernel,
        "middle",
        [
            jax.ShapeDtypeStruct((nodes, f_hid), jnp.bfloat16),
            of_blocks(sent_blocks),
        ],
        0,
        weight,
        cotangent,
        *parts,
    )

    (send,) = kernel_call(
        collect_kernel,
        "collect",
        [of_blocks(sent_blocks + own_blocks)],
        0,
        send,
        shift(send, "zh", 1),
    )
    near = [send] + [shift(send, "y", by) for by in (1, 2, 3)]
    (total,) = kernel_call(
        backward_near_kernel,
        "backward_near",
        [of_blocks(col_blocks, jnp.float32)],
        1,
        plan_b,
        held,
        *near[:2],
        scratch=[pltpu.VMEM((2 * each, BS, BS), jnp.bfloat16)],
    )
    half = col_blocks // 2
    sib, grad = kernel_call(
        backward_sib_kernel,
        "backward_sib",
        [of_blocks(half), of_blocks(sent_blocks - own_blocks)],
        1,
        plan_b,
        held,
        *near[2:],
        total,
        *near[:2],
        scratch=[pltpu.VMEM((2 * each, BS, BS), jnp.bfloat16), sums(half)],
    )
    other_sib, other_grad = swap_core(sib), swap_core(grad)
    (own,) = kernel_call(
        backward_own_kernel,
        "backward_own",
        [of_blocks(half)],
        1,
        plan_b,
        held,
        *near[2:],
        total,
        scratch=[pltpu.VMEM((2 * each, BS, BS), jnp.bfloat16), sums(half)],
    )
    other_sib, other_grad, own = lax.optimization_barrier((other_sib, other_grad, own))
    send = pair(own, other_sib, grad, other_grad, n_half)
    got = lax.all_to_all(send.reshape(-1, BS), ("zl", "x"), 0, 0, tiled=True)
    grad_features, grad_weight = last(got.reshape(send.shape), nodes, f_in, f_hid)
    return hidden, grad_weight, grad_features


def solution(mesh):
    fine = Mesh(mesh.devices.reshape(2, 4, 2, 2, 4), AXES)
    nodes = P(AXES, None)
    mapped = jax.shard_map(
        local,
        mesh=fine,
        in_specs=(
            nodes,
            P(),
            P(ROW, COL, None, None, None),
            P(ROW, COL, None),
            P(ROW, COL, None),
            P(ROW, COL),
            nodes,
        ),
        out_specs=(nodes, P(), nodes),
        check_vma=False,
    )
    return mapped
```

```python
import functools

import jax
import jax.numpy as jnp
from jax import lax
from jax.experimental import pallas as pl
from jax.experimental.pallas import tpu as pltpu
from jax.sharding import Mesh, PartitionSpec as P

AXES = ("zl", "x", "core", "zh", "y")
ROW = ("zl", "x", "core")
COL = ("zh", "y")
BS = 128
SHIFT = 10
FORWARD = (2, 32)
BACKWARD = (2, 32)
LIMIT = 24 << 20
CHUNK = 16
SMALL = pl.CostEstimate(flops=BS, bytes_accessed=BS, transcendentals=0)


def smem():
    return pl.BlockSpec(memory_space=pltpu.SMEM)


def vmem():
    return pl.BlockSpec(memory_space=pltpu.VMEM)


def hbm():
    return pl.BlockSpec(memory_space=pltpu.HBM)


def iota(shape, dim):
    return lax.broadcasted_iota(jnp.int32, shape, dim)


def places_of(slots, bounds, form):
    group, unroll = form
    groups = (slots + bounds[-1] * (group - 1)) // group
    groups += (len(bounds) - 1) * (unroll - 1)
    return -(-groups // 128) * 128 * group


def plan_size(places, form):
    return places + places // form[0] + 128


def places_in(plan, form):
    group, _ = form
    return (plan.shape[1] - 128) // (group + 1) * group


def make_plan(key, bounds, other, live, form, plan):
    group, unroll = form
    n_keys = bounds[-1]
    slots = key.shape[1]
    places = places_in(plan, form)
    targets = places // group
    here = (iota((n_keys, slots), 0) == key) & live
    marks = jnp.where(here, 1.0, 0.0)
    earlier = iota((slots, slots), 0) < iota((slots, slots), 1)
    rank = jnp.dot(
        marks.astype(jnp.bfloat16),
        jnp.where(earlier, 1.0, 0.0).astype(jnp.bfloat16),
        preferred_element_type=jnp.float32,
    )
    count = jnp.sum(marks, axis=1, keepdims=True).astype(jnp.int32)
    groups = lax.div(count + (group - 1), group)
    lower = iota((n_keys, n_keys), 1) < iota((n_keys, n_keys), 0)
    start = jnp.dot(
        jnp.where(lower, 1.0, 0.0).astype(jnp.bfloat16),
        jnp.broadcast_to(groups, (n_keys, 128)).astype(jnp.bfloat16),
        preferred_element_type=jnp.float32,
    )[:, :1].astype(jnp.int32)
    name = iota((n_keys, 1), 0)
    done = turns = jnp.zeros((1, 1), jnp.int32)
    ends = []
    for lo, hi in zip(bounds, bounds[1:]):
        inside = (name >= lo) & (name < hi)
        start = start + jnp.where(inside, turns * unroll - done, 0)
        here_now = jnp.sum(jnp.where(inside, groups, 0), axis=0, keepdims=True)
        done = done + here_now
        turns = turns + lax.div(here_now + (unroll - 1), unroll)
        ends.append(turns)
    place = jnp.where(here, rank.astype(jnp.int32) + start * group, 0)
    place = jnp.where(live, jnp.sum(place, axis=0, keepdims=True), -1)
    hit = iota((places, slots), 0) == place
    hit = jnp.where(hit, 1.0, 0.0).astype(jnp.bfloat16)
    row = iota((8, slots), 0)
    ids = iota((8, slots), 1) - slots
    low = ids & 127
    values = jnp.where(row == 1, ids - low, jnp.where(row == 2, other, 0))
    values = jnp.where(row == 0, low, values)
    found = lax.dot_general(
        values.astype(jnp.float32).astype(jnp.bfloat16),
        hit,
        (((1,), (1,)), ((), ())),
        preferred_element_type=jnp.float32,
    ).astype(jnp.int32)
    at = iota((n_keys, targets), 1)
    inside = (start <= at) & (at < start + groups)
    names = iota((n_keys, targets), 0)
    base = jnp.zeros_like(names)
    for lo in bounds[1:-1]:
        base = jnp.where(names >= lo, lo, base)
    names = names - base
    tile = found[0:1] + found[1:2] + slots
    plan[0:1, 0:places] = tile + (found[2:3] << SHIFT)
    plan[0:1, places : places + targets] = jnp.sum(
        jnp.where(inside, names, 0), axis=0, keepdims=True
    )
    lane = iota((1, 128), 1)
    last = jnp.zeros((1, 128), jnp.int32)
    for n, end in enumerate(ends):
        last = jnp.where(lane == n + 1, end, last)
    plan[0:1, places + targets :] = last


def around(parts):
    return (parts[0] + parts[2]) + (parts[1] + parts[3])


def divided(value, by, most):
    return sum(jnp.where(value >= by * t, 1, 0) for t in range(1, most // by + 1))


def plan_kernel(
    sizes, where, count, rows, cols, tiles, plan_f, plan_b, held, row_in, col_in, sem
):
    lo, hi = chunks_of(count, tiles, 0)

    copies = [
        pltpu.make_async_copy(rows, row_in, sem.at[0]),
        pltpu.make_async_copy(cols, col_in, sem.at[1]),
    ]
    for copy in copies:
        copy.start()

    @pl.loop(lo, hi)
    def _(i):
        chunk_copy(tiles, held, sem.at[2], i).start()

    held[tiles.shape[0]] = jnp.zeros((BS, BS), jnp.bfloat16)
    for copy in copies:
        copy.wait()
    own_blocks, row_blocks, col_blocks = sizes
    core, x, zl, y, zh = [where[i] for i in range(5)]
    row, col = row_in[...], col_in[...]
    live = iota(row.shape, 1) < count[0, 0]
    owner = divided(col, own_blocks, col_blocks - 1)
    inner = col - owner * own_blocks
    side = (owner & 1) ^ core
    half = col_blocks // 2
    owner = owner >> 1
    turned = ((owner >> 2) ^ zl) * 4 + ((x - (owner & 3)) & 3)
    spot = side * half + turned * own_blocks + inner
    ahead = ((owner & 3) - x) & 3
    dest = (1 - side) * half + (ahead * 2 + ((owner >> 2) ^ zl)) * own_blocks + inner

    owner = divided(row, own_blocks, row_blocks - 1)
    inner = row - owner * own_blocks
    inner = inner + ((owner >> 2) ^ zh) * own_blocks
    each = row_blocks // 4
    later = jnp.where(iota(row.shape, 1) >= row.shape[1] // 2, 2, 0)
    ahead = ((owner & 3) - y) & 3
    turn = jnp.where(ahead == 2, later, jnp.where(ahead == 1, later + 1, 4))
    key = jnp.where(ahead == 0, 5, turn) * each + inner
    make_plan(key, forward_bounds(sizes), spot, live, FORWARD, plan_f)
    behind = (y - (owner & 3)) & 3
    spot = (behind & 1) * each + inner
    key = dest + jnp.where(behind >= 2, col_blocks, 0)
    make_plan(key, backward_bounds(sizes), spot, live, BACKWARD, plan_b)

    @pl.loop(lo, hi)
    def _(i):
        chunk_copy(tiles, held, sem.at[2], i).wait()


def forward_bounds(sizes):
    each = sizes[1] // 4
    return (0, 2 * each, 4 * each, 5 * each, 6 * each)


def backward_bounds(sizes):
    columns = sizes[2]
    return (0, columns, columns + columns // 2, 2 * columns)


def make_plans(sizes, where, count, rows, cols, tiles):
    slots = rows.shape[1]
    places_f = places_of(slots, forward_bounds(sizes), FORWARD)
    places_b = places_of(slots, backward_bounds(sizes), BACKWARD)
    return pl.pallas_call(
        functools.partial(plan_kernel, sizes),
        out_shape=(
            jax.ShapeDtypeStruct((1, plan_size(places_f, FORWARD)), jnp.int32),
            jax.ShapeDtypeStruct((1, plan_size(places_b, BACKWARD)), jnp.int32),
            pltpu.VMEM((tiles.shape[0] + 1, BS, BS), tiles.dtype),
        ),
        in_specs=[smem()] * 2 + [hbm()] * 3,
        out_specs=(vmem(),) * 3,
        scratch_shapes=[pltpu.VMEM(rows.shape, jnp.int32)] * 2
        + [pltpu.SemaphoreType.DMA((3,))],
        compiler_params=pltpu.CompilerParams(vmem_limit_bytes=LIMIT),
        cost_estimate=pl.CostEstimate(
            flops=0, bytes_accessed=tiles.size, transcendentals=0
        ),
        name="make_plans",
    )(where, count, rows, cols, tiles)


def chunks_of(count, tiles, part):
    most = tiles.shape[0] // CHUNK // 2
    live = lax.div(count[0, 0] + (CHUNK - 1), CHUNK)
    return part * most, jnp.minimum(live, (part + 1) * most)


def chunk_copy(tiles, held, sem, i):
    at = pl.ds(pl.multiple_of(i * CHUNK, CHUNK), CHUNK)
    return pltpu.make_async_copy(tiles.at[at], held.at[at], sem)


def fetch(plan, here, sem):
    copy = pltpu.make_async_copy(plan, here, sem)
    copy.start()
    return copy


def multiply(plan, phases, form, tiles, source, tile_first, total):
    group, unroll = form
    places = places_in(plan, form)
    targets = places // group
    lo, hi = [plan[0, places + targets + phase] for phase in phases]

    @pl.loop(lo, hi)
    def _(turn):
        for u in range(unroll):
            at = turn * unroll + u
            spots = [plan[0, at * group + i] for i in range(group)]
            left = [tiles[spot & ((1 << SHIFT) - 1)] for spot in spots]
            right = [source[spot >> SHIFT] for spot in spots]
            if not tile_first:
                left, right = right, left
            total[plan[0, places + at]] += jnp.dot(
                jnp.concatenate(left, axis=1),
                jnp.concatenate(right, axis=0),
                preferred_element_type=jnp.float32,
            )


def forward_first_kernel(count, packed, tiles, _, *refs):
    blocks, (out, after, held, feats, plan, plan_sem, total, sem) = refs[:-8], refs[-8:]
    coming = fetch(packed, plan, plan_sem)
    lo, hi = chunks_of(count, tiles, 1)

    @pl.loop(lo, hi)
    def _(i):
        chunk_copy(tiles, held, sem, i).start()

    each = blocks[0].shape[0]
    for n, block in enumerate(blocks):
        feats[n * each : (n + 1) * each] = block[...]
    total[...] = jnp.zeros_like(total)

    coming.wait()
    multiply(plan, (0, 1), FORWARD, held, feats, True, total)

    @pl.loop(lo, hi)
    def _(i):
        chunk_copy(tiles, held, sem, i).wait()

    multiply(plan, (1, 2), FORWARD, held, feats, True, total)
    half = out.shape[0]
    out[...] = total[0:half].astype(jnp.bfloat16)
    after[...] = total[half : 2 * half].astype(jnp.bfloat16)


def forward_next_kernel(phase, packed, held, feats, out, plan, sem, *scratch):
    coming = fetch(packed, plan, sem)
    total = scratch[0] if scratch else out
    total[...] = jnp.zeros_like(total)
    coming.wait()
    multiply(plan, (phase, phase + 1), FORWARD, held, feats, True, total)
    if scratch:
        out[...] = total[...].astype(jnp.bfloat16)


def put_sources(source, first, second):
    each = source.shape[0] // 2
    source[0:each] = first[0:each]
    source[each : 2 * each] = second[0:each]


def backward_near_kernel(packed, held, first, second, total, plan, sem, source):
    coming = fetch(packed, plan, sem)
    put_sources(source, first, second)
    total[...] = jnp.zeros_like(total)
    coming.wait()
    multiply(plan, (0, 1), BACKWARD, held, source, False, total)


def backward_sib_kernel(
    packed, held, first, second, before, near, next_, out, both, plan, sem, source, total
):
    coming = fetch(packed, plan, sem)
    put_sources(source, first, second)
    each = source.shape[0] // 2
    parts = [block[each:].astype(jnp.float32) for block in (near, next_, first, second)]
    both[...] = around(parts).astype(jnp.bfloat16)
    total[...] = before[0 : total.shape[0]]
    coming.wait()
    multiply(plan, (1, 2), BACKWARD, held, source, False, total)
    out[...] = total[...].astype(jnp.bfloat16)


def backward_own_kernel(
    packed, held, first, second, before, out, plan, sem, source, total
):
    coming = fetch(packed, plan, sem)
    put_sources(source, first, second)
    half = total.shape[0]
    total[...] = before[half : 2 * half]
    coming.wait()
    multiply(plan, (2, 3), BACKWARD, held, source, False, total)
    out[...] = total[...].astype(jnp.bfloat16)


def add_kernel(total, first, second, third, keep, send):
    parts = [part[...].astype(jnp.float32) for part in (first, second, third)]
    total = total[...] + sum(parts)
    each = keep.shape[0]
    keep[...] = total[0:each]
    send[...] = total[each : 2 * each].astype(jnp.bfloat16)


def collect_kernel(own, other, send):
    each = send.shape[0] - own.shape[0]
    send[0:each] = own[0:each]
    send[each : 2 * each] = other[0:each]
    grad = own[each:].astype(jnp.float32) + other[each:].astype(jnp.float32)
    send[2 * each :] = grad.astype(jnp.bfloat16)


def kernel_call(kernel, name, outs, n_smem, *args, scratch=(), aliases={}, in_hbm=()):
    specs = [smem() if n < n_smem else vmem() for n in range(len(args))]
    specs = [hbm() if n in in_hbm else spec for n, spec in enumerate(specs)]
    return pl.pallas_call(
        kernel,
        out_shape=tuple(outs),
        in_specs=specs,
        out_specs=(vmem(),) * len(outs),
        scratch_shapes=list(scratch),
        input_output_aliases=aliases,
        compiler_params=pltpu.CompilerParams(vmem_limit_bytes=LIMIT),
        cost_estimate=SMALL,
        name=name,
    )(*args)


def of_blocks(n, dtype=jnp.bfloat16):
    return jax.ShapeDtypeStruct((n, BS, BS), dtype)


def plan_space(plan):
    return [pltpu.SMEM(plan.shape, jnp.int32), pltpu.SemaphoreType.DMA]


def sums(n):
    return pltpu.VMEM((n, BS, BS), jnp.float32)


def middle_kernel(weight, cot, *refs):
    parts, (hidden, send) = refs[:-2], refs[-2:]
    agg = sum(part[...].astype(jnp.float32) for part in parts).astype(jnp.bfloat16)
    w = weight[...]
    pre = jnp.dot(agg, w, preferred_element_type=jnp.float32)
    scale = 0.7978845608028654
    inner = scale * (pre + 0.044715 * (pre * pre * pre))
    t = jnp.tanh(inner)
    half = 0.5 * (1.0 + t)
    hidden[...] = (pre * half).astype(jnp.bfloat16)
    slope = half + 0.5 * pre * (1.0 - t * t) * (
        scale * (1.0 + (3 * 0.044715) * (pre * pre))
    )
    delta = (cot[...].astype(jnp.float32) * slope).astype(jnp.bfloat16)
    grad = lax.dot_general(
        agg, delta, (((0,), (0,)), ((), ())), preferred_element_type=jnp.float32
    ).astype(jnp.bfloat16)
    each = agg.shape[0] // BS
    for j in range(each):
        send[j] = lax.dot_general(
            w,
            delta[j * BS : (j + 1) * BS],
            (((1,), (1,)), ((), ())),
            preferred_element_type=jnp.float32,
        ).astype(jnp.bfloat16)
    for i in range(grad.shape[1] // BS):
        send[each + i] = grad[:, i * BS : (i + 1) * BS]


def pair_kernel(own, sib, grad, other_grad, *sends):
    both = grad[...].astype(jnp.float32) + other_grad[...].astype(jnp.float32)
    each = own.shape[0] // len(sends)
    for n, send in enumerate(sends):
        at = slice(n * each, (n + 1) * each)
        total = own[at].astype(jnp.float32) + sib[at].astype(jnp.float32)
        send[0:each] = total.astype(jnp.bfloat16)
        send[each:] = both.astype(jnp.bfloat16)


def gather_kernel(first, second, third, fourth, keep, send):
    parts = (first, second, third, fourth)
    each = keep.shape[0]
    keep[...] = around([part[0:each].astype(jnp.float32) for part in parts])
    rest = around([part[each:].astype(jnp.float32) for part in parts])
    send[...] = rest.astype(jnp.bfloat16)


def last_kernel(keep, send, got, grad_features, grad_weight):
    each = keep.shape[0]
    for j in range(each):
        total = keep[j] + got[j].astype(jnp.float32)
        grad_features[j * BS : (j + 1) * BS] = total.T.astype(jnp.bfloat16)
    for i in range(grad_weight.shape[1] // BS):
        total = send[each + i].astype(jnp.float32) + got[each + i].astype(jnp.float32)
        grad_weight[:, i * BS : (i + 1) * BS] = total


def swap_core(value):
    return shift(value, "core", 1)


def shift(value, axis, by):
    n = lax.axis_size(axis)
    return lax.ppermute(value, axis, [(i, (i + by) % n) for i in range(n)])


def local(features, weight, tile_values, tile_rows, tile_cols, tile_count, cotangent):
    f_in, f_hid = weight.shape
    nodes = features.shape[0]
    own_blocks = nodes // BS
    n_x, n_zl = lax.axis_size("x"), lax.axis_size("zl")
    n_col = lax.axis_size(COL)
    n_half = n_x * n_zl
    row_blocks = own_blocks * n_col
    col_blocks = own_blocks * n_half * 2
    tiles = pltpu.with_memory_space_constraint(tile_values[0, 0], pltpu.HBM)
    sent_blocks = own_blocks + f_in * f_hid // (BS * BS)
    sizes = (own_blocks, row_blocks, col_blocks)
    rows = pltpu.with_memory_space_constraint(tile_rows[0], pltpu.HBM)
    cols = pltpu.with_memory_space_constraint(tile_cols[0], pltpu.HBM)
    where = jnp.stack([lax.axis_index(a) for a in ("core", "x", "zl", "y", "zh")])

    near = [features] + [shift(features, "x", by) for by in range(1, n_x)]
    far = [shift(features, "zl", 1)]
    plan_f, plan_b, held = make_plans(sizes, where, tile_count, rows, cols, tiles)
    near, far, held = lax.optimization_barrier((near, far, held))
    far += [shift(near[1], "zl", 1), shift(far[0], "x", 2), shift(near[3], "zl", 1)]
    other = [swap_core(block) for block in near + far]
    blocks = [b.reshape(own_blocks, BS, f_in) for b in near + far + other]

    each = row_blocks // 4
    first, second, held, feats = kernel_call(
        forward_first_kernel,
        "forward_first",
        [
            of_blocks(each),
            of_blocks(each),
            pltpu.VMEM(held.shape, held.dtype),
            of_blocks(col_blocks),
        ],
        1,
        tile_count,
        plan_f,
        tiles,
        held,
        *blocks,
        scratch=plan_space(plan_f) + [sums(2 * each), pltpu.SemaphoreType.DMA],
        aliases={3: 2},
        in_hbm=(2,),
    )
    got = [shift(first, "y", 2), shift(second, "y", 1)]
    (third,) = kernel_call(
        functools.partial(forward_next_kernel, 2),
        "forward_next",
        [of_blocks(each)],
        0,
        plan_f,
        held,
        feats,
        scratch=plan_space(plan_f) + [sums(each)],
    )
    got.append(shift(third, "y", 3))
    held, feats, third = lax.optimization_barrier((held, feats, third))
    (total,) = kernel_call(
        functools.partial(forward_next_kernel, 3),
        "forward_here",
        [of_blocks(each, jnp.float32)],
        0,
        plan_f,
        held,
        feats,
        scratch=plan_space(plan_f),
    )
    keep, send = kernel_call(
        add_kernel,
        "add",
        [of_blocks(own_blocks, jnp.float32), of_blocks(own_blocks)],
        0,
        total,
        *got,
    )
    parts = [part.reshape(nodes, f_in) for part in (keep, shift(send, "zh", 1))]
    hidden, send = kernel_call(
        middle_kernel,
        "middle",
        [
            jax.ShapeDtypeStruct((nodes, f_hid), jnp.bfloat16),
            of_blocks(sent_blocks),
        ],
        0,
        weight,
        cotangent,
        *parts,
    )

    (send,) = kernel_call(
        collect_kernel,
        "collect",
        [of_blocks(sent_blocks + own_blocks)],
        0,
        send,
        shift(send, "zh", 1),
    )
    near = [send] + [shift(send, "y", by) for by in (1, 2, 3)]
    (total,) = kernel_call(
        backward_near_kernel,
        "backward_near",
        [of_blocks(col_blocks, jnp.float32)],
        0,
        plan_b,
        held,
        *near[:2],
        scratch=plan_space(plan_b) + [pltpu.VMEM((2 * each, BS, BS), jnp.bfloat16)],
    )
    half = col_blocks // 2
    sib, grad = kernel_call(
        backward_sib_kernel,
        "backward_sib",
        [of_blocks(half), of_blocks(sent_blocks - own_blocks)],
        0,
        plan_b,
        held,
        *near[2:],
        total,
        *near[:2],
        scratch=plan_space(plan_b) + [pltpu.VMEM((2 * each, BS, BS), jnp.bfloat16), sums(half)],
    )
    other_sib, other_grad = swap_core(sib), swap_core(grad)
    (own,) = kernel_call(
        backward_own_kernel,
        "backward_own",
        [of_blocks(half)],
        0,
        plan_b,
        held,
        *near[2:],
        total,
        scratch=plan_space(plan_b) + [pltpu.VMEM((2 * each, BS, BS), jnp.bfloat16), sums(half)],
    )
    other_sib, other_grad, own = lax.optimization_barrier((other_sib, other_grad, own))
    n_grad = sent_blocks - own_blocks
    sends = kernel_call(
        pair_kernel,
        "pair",
        [of_blocks(2 * own_blocks + n_grad)] * 4,
        0,
        own,
        other_sib,
        grad,
        other_grad,
    )
    parts = [sends[0]] + [shift(sends[by], "x", by) for by in (1, 2, 3)]
    keep, send = kernel_call(
        gather_kernel,
        "gather",
        [of_blocks(own_blocks, jnp.float32), of_blocks(sent_blocks)],
        0,
        *parts,
    )
    grad_features, grad_weight = kernel_call(
        last_kernel,
        "last",
        [
            jax.ShapeDtypeStruct((nodes, f_in), jnp.bfloat16),
            jax.ShapeDtypeStruct((f_in, f_hid), jnp.float32),
        ],
        0,
        keep,
        send,
        shift(send, "zl", 1),
    )
    return hidden, grad_weight, grad_features


def solution(mesh):
    fine = Mesh(mesh.devices.reshape(2, 4, 2, 2, 4), AXES)
    nodes = P(AXES, None)
    mapped = jax.shard_map(
        local,
        mesh=fine,
        in_specs=(
            nodes,
            P(),
            P(ROW, COL, None, None, None),
            P(ROW, COL, None),
            P(ROW, COL, None),
            P(ROW, COL),
            nodes,
        ),
        out_specs=(nodes, P(), nodes),
        check_vma=False,
    )
    return mapped
```

```python
import functools

import jax
import jax.numpy as jnp
from jax import lax
from jax.experimental import pallas as pl
from jax.experimental.pallas import tpu as pltpu
from jax.sharding import Mesh, PartitionSpec as P

AXES = ("zl", "x", "core", "zh", "y")
ROW = ("zl", "x", "core")
COL = ("zh", "y")
BS = 128
SHIFT = 10
FORWARD = (2, 32)
BACKWARD = (2, 32)
LIMIT = 24 << 20
CHUNK = 16
SMALL = pl.CostEstimate(flops=BS, bytes_accessed=BS, transcendentals=0)


def smem():
    return pl.BlockSpec(memory_space=pltpu.SMEM)


def vmem():
    return pl.BlockSpec(memory_space=pltpu.VMEM)


def hbm():
    return pl.BlockSpec(memory_space=pltpu.HBM)


def iota(shape, dim):
    return lax.broadcasted_iota(jnp.int32, shape, dim)


def places_of(slots, bounds, form):
    group, unroll = form
    groups = (slots + bounds[-1] * (group - 1)) // group
    groups += (len(bounds) - 1) * (unroll - 1)
    return -(-groups // 128) * 128 * group


def plan_size(places, form):
    return places + places // form[0] + 128


def places_in(plan, form):
    group, _ = form
    return (plan.shape[1] - 128) // (group + 1) * group


def make_plan(key, bounds, other, live, form, plan):
    group, unroll = form
    n_keys = bounds[-1]
    slots = key.shape[1]
    places = places_in(plan, form)
    targets = places // group
    here = (iota((n_keys, slots), 0) == key) & live
    marks = jnp.where(here, 1.0, 0.0)
    earlier = iota((slots, slots), 0) < iota((slots, slots), 1)
    rank = jnp.dot(
        marks.astype(jnp.bfloat16),
        jnp.where(earlier, 1.0, 0.0).astype(jnp.bfloat16),
        preferred_element_type=jnp.float32,
    )
    count = jnp.sum(marks, axis=1, keepdims=True).astype(jnp.int32)
    groups = lax.div(count + (group - 1), group)
    lower = iota((n_keys, n_keys), 1) < iota((n_keys, n_keys), 0)
    start = jnp.dot(
        jnp.where(lower, 1.0, 0.0).astype(jnp.bfloat16),
        jnp.broadcast_to(groups, (n_keys, 128)).astype(jnp.bfloat16),
        preferred_element_type=jnp.float32,
    )[:, :1].astype(jnp.int32)
    name = iota((n_keys, 1), 0)
    done = turns = jnp.zeros((1, 1), jnp.int32)
    ends = []
    for lo, hi in zip(bounds, bounds[1:]):
        inside = (name >= lo) & (name < hi)
        start = start + jnp.where(inside, turns * unroll - done, 0)
        here_now = jnp.sum(jnp.where(inside, groups, 0), axis=0, keepdims=True)
        done = done + here_now
        turns = turns + lax.div(here_now + (unroll - 1), unroll)
        ends.append(turns)
    place = jnp.where(here, rank.astype(jnp.int32) + start * group, 0)
    place = jnp.where(live, jnp.sum(place, axis=0, keepdims=True), -1)
    hit = iota((places, slots), 0) == place
    hit = jnp.where(hit, 1.0, 0.0).astype(jnp.bfloat16)
    row = iota((8, slots), 0)
    ids = iota((8, slots), 1) - slots
    low = ids & 127
    values = jnp.where(row == 1, ids - low, jnp.where(row == 2, other, 0))
    values = jnp.where(row == 0, low, values)
    found = lax.dot_general(
        values.astype(jnp.float32).astype(jnp.bfloat16),
        hit,
        (((1,), (1,)), ((), ())),
        preferred_element_type=jnp.float32,
    ).astype(jnp.int32)
    at = iota((n_keys, targets), 1)
    inside = (start <= at) & (at < start + groups)
    names = iota((n_keys, targets), 0)
    base = jnp.zeros_like(names)
    for lo in bounds[1:-1]:
        base = jnp.where(names >= lo, lo, base)
    names = names - base
    tile = found[0:1] + found[1:2] + slots
    plan[0:1, 0:places] = tile + (found[2:3] << SHIFT)
    plan[0:1, places : places + targets] = jnp.sum(
        jnp.where(inside, names, 0), axis=0, keepdims=True
    )
    lane = iota((1, 128), 1)
    last = jnp.zeros((1, 128), jnp.int32)
    for n, end in enumerate(ends):
        last = jnp.where(lane == n + 1, end, last)
    plan[0:1, places + targets :] = last


def around(parts):
    return (parts[0] + parts[2]) + (parts[1] + parts[3])


def divided(value, by, most):
    return sum(jnp.where(value >= by * t, 1, 0) for t in range(1, most // by + 1))


def plan_kernel(
    sizes, where, count, rows, cols, tiles, plan_f, plan_b, held, row_in, col_in, sem
):
    lo, hi = chunks_of(count, tiles, 0)

    copies = [
        pltpu.make_async_copy(rows, row_in, sem.at[0]),
        pltpu.make_async_copy(cols, col_in, sem.at[1]),
    ]
    for copy in copies:
        copy.start()

    @pl.loop(lo, hi)
    def _(i):
        chunk_copy(tiles, held, sem.at[2], i).start()

    held[tiles.shape[0]] = jnp.zeros((BS, BS), jnp.bfloat16)
    for copy in copies:
        copy.wait()
    own_blocks, row_blocks, col_blocks = sizes
    core, x, zl, y, zh = [where[i] for i in range(5)]
    row, col = row_in[...], col_in[...]
    live = iota(row.shape, 1) < count[0, 0]
    owner = divided(col, own_blocks, col_blocks - 1)
    inner = col - owner * own_blocks
    side = (owner & 1) ^ core
    half = col_blocks // 2
    owner = owner >> 1
    turned = ((owner >> 2) ^ zl) * 4 + ((x - (owner & 3)) & 3)
    spot = side * half + turned * own_blocks + inner
    ahead = ((owner & 3) - x) & 3
    order = (1 - ((owner >> 2) ^ zl)) * 4 + ahead
    dest = (1 - side) * half + order * own_blocks + inner

    owner = divided(row, own_blocks, row_blocks - 1)
    inner = row - owner * own_blocks
    away = (owner >> 2) ^ zh
    each = row_blocks // 4
    later = jnp.where(iota(row.shape, 1) >= row.shape[1] // 2, 1, 0)
    turn = jnp.where(away == 1, later, 2)
    key = (turn * 4 + (((owner & 3) - y) & 3)) * own_blocks + inner
    make_plan(key, forward_bounds(sizes), spot, live, FORWARD, plan_f)
    behind = (y - (owner & 3)) & 3
    spot = (behind & 1) * each + away * own_blocks + inner
    key = dest + jnp.where(behind >= 2, col_blocks, 0)
    make_plan(key, backward_bounds(sizes), spot, live, BACKWARD, plan_b)

    @pl.loop(lo, hi)
    def _(i):
        chunk_copy(tiles, held, sem.at[2], i).wait()


def forward_bounds(sizes):
    each = sizes[1] // 4
    return (0, 2 * each, 4 * each, 6 * each)


def backward_bounds(sizes):
    columns = sizes[2]
    return (0, columns, columns + columns // 2, 2 * columns)


def make_plans(sizes, where, count, rows, cols, tiles):
    slots = rows.shape[1]
    places_f = places_of(slots, forward_bounds(sizes), FORWARD)
    places_b = places_of(slots, backward_bounds(sizes), BACKWARD)
    return pl.pallas_call(
        functools.partial(plan_kernel, sizes),
        out_shape=(
            jax.ShapeDtypeStruct((1, plan_size(places_f, FORWARD)), jnp.int32),
            jax.ShapeDtypeStruct((1, plan_size(places_b, BACKWARD)), jnp.int32),
            pltpu.VMEM((tiles.shape[0] + 1, BS, BS), tiles.dtype),
        ),
        in_specs=[smem()] * 2 + [hbm()] * 3,
        out_specs=(vmem(),) * 3,
        scratch_shapes=[pltpu.VMEM(rows.shape, jnp.int32)] * 2
        + [pltpu.SemaphoreType.DMA((3,))],
        compiler_params=pltpu.CompilerParams(vmem_limit_bytes=LIMIT),
        cost_estimate=pl.CostEstimate(
            flops=0, bytes_accessed=tiles.size, transcendentals=0
        ),
        name="make_plans",
    )(where, count, rows, cols, tiles)


def chunks_of(count, tiles, part):
    most = tiles.shape[0] // CHUNK // 2
    live = lax.div(count[0, 0] + (CHUNK - 1), CHUNK)
    return part * most, jnp.minimum(live, (part + 1) * most)


def chunk_copy(tiles, held, sem, i):
    at = pl.ds(pl.multiple_of(i * CHUNK, CHUNK), CHUNK)
    return pltpu.make_async_copy(tiles.at[at], held.at[at], sem)


def fetch(plan, here, sem):
    copy = pltpu.make_async_copy(plan, here, sem)
    copy.start()
    return copy


def multiply(plan, phases, form, tiles, source, tile_first, total):
    group, unroll = form
    places = places_in(plan, form)
    targets = places // group
    lo, hi = [plan[0, places + targets + phase] for phase in phases]

    @pl.loop(lo, hi)
    def _(turn):
        for u in range(unroll):
            at = turn * unroll + u
            spots = [plan[0, at * group + i] for i in range(group)]
            left = [tiles[spot & ((1 << SHIFT) - 1)] for spot in spots]
            right = [source[spot >> SHIFT] for spot in spots]
            if not tile_first:
                left, right = right, left
            total[plan[0, places + at]] += jnp.dot(
                jnp.concatenate(left, axis=1),
                jnp.concatenate(right, axis=0),
                preferred_element_type=jnp.float32,
            )


def forward_away_kernel(count, packed, tiles, _, *refs):
    blocks, outs, refs = refs[:-10], refs[-10:-6], refs[-6:]
    held, feats, plan, plan_sem, total, sem = refs
    coming = fetch(packed, plan, plan_sem)
    lo, hi = chunks_of(count, tiles, 1)

    @pl.loop(lo, hi)
    def _(i):
        chunk_copy(tiles, held, sem, i).start()

    each = blocks[0].shape[0]
    for n, block in enumerate(blocks):
        feats[n * each : (n + 1) * each] = block[...]
    total[...] = jnp.zeros_like(total)

    coming.wait()
    multiply(plan, (0, 1), FORWARD, held, feats, True, total)

    @pl.loop(lo, hi)
    def _(i):
        chunk_copy(tiles, held, sem, i).wait()

    multiply(plan, (1, 2), FORWARD, held, feats, True, total)
    for n, out in enumerate(outs):
        out[...] = total[n * out.shape[0] : (n + 1) * out.shape[0]].astype(out.dtype)


def forward_here_kernel(packed, held, feats, *refs):
    outs, (plan, sem, total) = refs[:4], refs[4:]
    coming = fetch(packed, plan, sem)
    total[...] = jnp.zeros_like(total)
    coming.wait()
    multiply(plan, (2, 3), FORWARD, held, feats, True, total)
    for n, out in enumerate(outs):
        out[...] = total[n * out.shape[0] : (n + 1) * out.shape[0]].astype(out.dtype)


def put_sources(source, first, second):
    each = source.shape[0] // 2
    source[0:each] = first[0:each]
    source[each : 2 * each] = second[0:each]


def backward_near_kernel(packed, held, first, second, total, plan, sem, source):
    coming = fetch(packed, plan, sem)
    put_sources(source, first, second)
    total[...] = jnp.zeros_like(total)
    coming.wait()
    multiply(plan, (0, 1), BACKWARD, held, source, False, total)


def backward_sib_kernel(
    packed, held, first, second, before, near, next_, out, both, plan, sem, source, total
):
    coming = fetch(packed, plan, sem)
    put_sources(source, first, second)
    each = source.shape[0] // 2
    parts = [block[each:].astype(jnp.float32) for block in (near, next_, first, second)]
    both[...] = around(parts).astype(jnp.bfloat16)
    total[...] = before[0 : total.shape[0]]
    coming.wait()
    multiply(plan, (1, 2), BACKWARD, held, source, False, total)
    out[...] = total[...].astype(jnp.bfloat16)


def backward_own_kernel(
    packed, held, first, second, before, out, plan, sem, source, total
):
    coming = fetch(packed, plan, sem)
    put_sources(source, first, second)
    half = total.shape[0]
    total[...] = before[half : 2 * half]
    coming.wait()
    multiply(plan, (2, 3), BACKWARD, held, source, False, total)
    out[...] = total[...].astype(jnp.bfloat16)


def add_kernel(first, second, third, fourth, send):
    parts = [part[...].astype(jnp.float32) for part in (first, second, third, fourth)]
    send[...] = sum(parts).astype(jnp.bfloat16)


def collect_kernel(own, other, send):
    each = send.shape[0] - own.shape[0]
    send[0:each] = own[0:each]
    send[each : 2 * each] = other[0:each]
    grad = own[each:].astype(jnp.float32) + other[each:].astype(jnp.float32)
    send[2 * each :] = grad.astype(jnp.bfloat16)


def kernel_call(kernel, name, outs, n_smem, *args, scratch=(), aliases={}, in_hbm=()):
    specs = [smem() if n < n_smem else vmem() for n in range(len(args))]
    specs = [hbm() if n in in_hbm else spec for n, spec in enumerate(specs)]
    return pl.pallas_call(
        kernel,
        out_shape=tuple(outs),
        in_specs=specs,
        out_specs=(vmem(),) * len(outs),
        scratch_shapes=list(scratch),
        input_output_aliases=aliases,
        compiler_params=pltpu.CompilerParams(vmem_limit_bytes=LIMIT),
        cost_estimate=SMALL,
        name=name,
    )(*args)


def of_blocks(n, dtype=jnp.bfloat16):
    return jax.ShapeDtypeStruct((n, BS, BS), dtype)


def plan_space(plan):
    return [pltpu.SMEM(plan.shape, jnp.int32), pltpu.SemaphoreType.DMA]


def sums(n):
    return pltpu.VMEM((n, BS, BS), jnp.float32)


def middle_kernel(weight, cot, *refs):
    parts, (hidden, send) = refs[:-2], refs[-2:]
    agg = sum(part[...].astype(jnp.float32) for part in parts).astype(jnp.bfloat16)
    w = weight[...]
    pre = jnp.dot(agg, w, preferred_element_type=jnp.float32)
    scale = 0.7978845608028654
    inner = scale * (pre + 0.044715 * (pre * pre * pre))
    t = jnp.tanh(inner)
    half = 0.5 * (1.0 + t)
    hidden[...] = (pre * half).astype(jnp.bfloat16)
    slope = half + 0.5 * pre * (1.0 - t * t) * (
        scale * (1.0 + (3 * 0.044715) * (pre * pre))
    )
    delta = (cot[...].astype(jnp.float32) * slope).astype(jnp.bfloat16)
    grad = lax.dot_general(
        agg, delta, (((0,), (0,)), ((), ())), preferred_element_type=jnp.float32
    ).astype(jnp.bfloat16)
    each = agg.shape[0] // BS
    for j in range(each):
        send[j] = lax.dot_general(
            w,
            delta[j * BS : (j + 1) * BS],
            (((1,), (1,)), ((), ())),
            preferred_element_type=jnp.float32,
        ).astype(jnp.bfloat16)
    for i in range(grad.shape[1] // BS):
        send[each + i] = grad[:, i * BS : (i + 1) * BS]


def pair_kernel(own, sib, grad, other_grad, *sends):
    both = grad[...].astype(jnp.float32) + other_grad[...].astype(jnp.float32)
    each = own.shape[0] // len(sends)
    for n, send in enumerate(sends):
        at = slice(n * each, (n + 1) * each)
        total = own[at].astype(jnp.float32) + sib[at].astype(jnp.float32)
        send[0:each] = total.astype(jnp.bfloat16)
        if n < len(sends) // 2:
            send[each:] = both.astype(jnp.bfloat16)


def gather_kernel(first, second, third, fourth, send):
    parts = (first, second, third, fourth)
    send[...] = around([part[...].astype(jnp.float32) for part in parts]).astype(
        jnp.bfloat16
    )


def last_kernel(send, got, first, second, third, fourth, grad_features, grad_weight):
    parts = (first, second, third, fourth)
    each = first.shape[0]
    for j in range(each):
        total = around([part[j].astype(jnp.float32) for part in parts])
        total = total + got[j].astype(jnp.float32)
        grad_features[j * BS : (j + 1) * BS] = total.T.astype(jnp.bfloat16)
    for i in range(grad_weight.shape[1] // BS):
        total = send[each + i].astype(jnp.float32) + got[each + i].astype(jnp.float32)
        grad_weight[:, i * BS : (i + 1) * BS] = total


def swap_core(value):
    return shift(value, "core", 1)


def shift(value, axis, by):
    n = lax.axis_size(axis)
    return lax.ppermute(value, axis, [(i, (i + by) % n) for i in range(n)])


def local(features, weight, tile_values, tile_rows, tile_cols, tile_count, cotangent):
    f_in, f_hid = weight.shape
    nodes = features.shape[0]
    own_blocks = nodes // BS
    n_x, n_zl = lax.axis_size("x"), lax.axis_size("zl")
    n_col = lax.axis_size(COL)
    n_half = n_x * n_zl
    row_blocks = own_blocks * n_col
    col_blocks = own_blocks * n_half * 2
    tiles = pltpu.with_memory_space_constraint(tile_values[0, 0], pltpu.HBM)
    sent_blocks = own_blocks + f_in * f_hid // (BS * BS)
    sizes = (own_blocks, row_blocks, col_blocks)
    rows = pltpu.with_memory_space_constraint(tile_rows[0], pltpu.HBM)
    cols = pltpu.with_memory_space_constraint(tile_cols[0], pltpu.HBM)
    where = jnp.stack([lax.axis_index(a) for a in ("core", "x", "zl", "y", "zh")])

    near = [features] + [shift(features, "x", by) for by in range(1, n_x)]
    far = [shift(features, "zl", 1)]
    plan_f, plan_b, held = make_plans(sizes, where, tile_count, rows, cols, tiles)
    near, far, held = lax.optimization_barrier((near, far, held))
    far += [shift(near[1], "zl", 1), shift(far[0], "x", 2), shift(near[3], "zl", 1)]
    other = [swap_core(block) for block in near + far]
    blocks = [b.reshape(own_blocks, BS, f_in) for b in near + far + other]

    each = row_blocks // 4
    *sends, held, feats = kernel_call(
        forward_away_kernel,
        "forward_away",
        [of_blocks(own_blocks, jnp.float32)]
        + [of_blocks(own_blocks)] * 3
        + [pltpu.VMEM(held.shape, held.dtype), of_blocks(col_blocks)],
        1,
        tile_count,
        plan_f,
        tiles,
        held,
        *blocks,
        scratch=plan_space(plan_f) + [sums(2 * each), pltpu.SemaphoreType.DMA],
        aliases={3: 4},
        in_hbm=(2,),
    )
    away = [sends[0]] + [shift(sends[by], "y", by) for by in (1, 2, 3)]
    sends = kernel_call(
        forward_here_kernel,
        "forward_here",
        [of_blocks(own_blocks, jnp.float32)] + [of_blocks(own_blocks)] * 3,
        0,
        plan_f,
        held,
        feats,
        scratch=plan_space(plan_f) + [sums(2 * each)],
    )
    here = [sends[0]] + [shift(sends[by], "y", by) for by in (1, 2, 3)]
    (send,) = kernel_call(add_kernel, "add", [of_blocks(own_blocks)], 0, *away)
    parts = [part.reshape(nodes, f_in) for part in here + [shift(send, "zh", 1)]]
    hidden, send = kernel_call(
        middle_kernel,
        "middle",
        [
            jax.ShapeDtypeStruct((nodes, f_hid), jnp.bfloat16),
            of_blocks(sent_blocks),
        ],
        0,
        weight,
        cotangent,
        *parts,
    )

    (send,) = kernel_call(
        collect_kernel,
        "collect",
        [of_blocks(sent_blocks + own_blocks)],
        0,
        send,
        shift(send, "zh", 1),
    )
    near = [send] + [shift(send, "y", by) for by in (1, 2, 3)]
    (total,) = kernel_call(
        backward_near_kernel,
        "backward_near",
        [of_blocks(col_blocks, jnp.float32)],
        0,
        plan_b,
        held,
        *near[:2],
        scratch=plan_space(plan_b) + [pltpu.VMEM((2 * each, BS, BS), jnp.bfloat16)],
    )
    half = col_blocks // 2
    sib, grad = kernel_call(
        backward_sib_kernel,
        "backward_sib",
        [of_blocks(half), of_blocks(sent_blocks - own_blocks)],
        0,
        plan_b,
        held,
        *near[2:],
        total,
        *near[:2],
        scratch=plan_space(plan_b) + [pltpu.VMEM((2 * each, BS, BS), jnp.bfloat16), sums(half)],
    )
    other_sib, other_grad = swap_core(sib), swap_core(grad)
    (own,) = kernel_call(
        backward_own_kernel,
        "backward_own",
        [of_blocks(half)],
        0,
        plan_b,
        held,
        *near[2:],
        total,
        scratch=plan_space(plan_b) + [pltpu.VMEM((2 * each, BS, BS), jnp.bfloat16), sums(half)],
    )
    other_sib, other_grad, own = lax.optimization_barrier((other_sib, other_grad, own))
    n_grad = sent_blocks - own_blocks
    sends = kernel_call(
        pair_kernel,
        "pair",
        [of_blocks(own_blocks + n_grad)] * 4 + [of_blocks(own_blocks)] * 4,
        0,
        own,
        other_sib,
        grad,
        other_grad,
    )
    away = [sends[0]] + [shift(sends[by], "x", by) for by in (2, 1, 3)]
    here = [sends[4]] + [shift(sends[4 + by], "x", by) for by in (2, 1, 3)]
    (send,) = kernel_call(
        gather_kernel,
        "gather",
        [of_blocks(sent_blocks)],
        0,
        away[0],
        away[2],
        away[1],
        away[3],
    )
    grad_features, grad_weight = kernel_call(
        last_kernel,
        "last",
        [
            jax.ShapeDtypeStruct((nodes, f_in), jnp.bfloat16),
            jax.ShapeDtypeStruct((f_in, f_hid), jnp.float32),
        ],
        0,
        send,
        shift(send, "zl", 1),
        here[0],
        here[2],
        here[1],
        here[3],
    )
    return hidden, grad_weight, grad_features


def solution(mesh):
    fine = Mesh(mesh.devices.reshape(2, 4, 2, 2, 4), AXES)
    nodes = P(AXES, None)
    mapped = jax.shard_map(
        local,
        mesh=fine,
        in_specs=(
            nodes,
            P(),
            P(ROW, COL, None, None, None),
            P(ROW, COL, None),
            P(ROW, COL, None),
            P(ROW, COL),
            nodes,
        ),
        out_specs=(nodes, P(), nodes),
        check_vma=False,
    )
    return mapped
```

```python
import functools

import jax
import jax.numpy as jnp
from jax import lax
from jax.experimental import pallas as pl
from jax.experimental.pallas import tpu as pltpu
from jax.sharding import Mesh, PartitionSpec as P

AXES = ("zl", "x", "core", "zh", "y")
ROW = ("zl", "x", "core")
COL = ("zh", "y")
BS = 128
SHIFT = 10
FORWARD = (2, 32)
BACKWARD = (2, 32)
LIMIT = 24 << 20
CHUNK = 16
SMALL = pl.CostEstimate(flops=BS, bytes_accessed=BS, transcendentals=0)


def smem():
    return pl.BlockSpec(memory_space=pltpu.SMEM)


def vmem():
    return pl.BlockSpec(memory_space=pltpu.VMEM)


def hbm():
    return pl.BlockSpec(memory_space=pltpu.HBM)


def iota(shape, dim):
    return lax.broadcasted_iota(jnp.int32, shape, dim)


def places_of(slots, bounds, form):
    group, unroll = form
    groups = (slots + bounds[-1] * (group - 1)) // group
    groups += (len(bounds) - 1) * (unroll - 1)
    return -(-groups // 128) * 128 * group


def plan_size(places, form):
    return places + places // form[0] + 128


def places_in(plan, form):
    group, _ = form
    return (plan.shape[1] - 128) // (group + 1) * group


def make_plan(key, bounds, other, live, form, plan):
    group, unroll = form
    n_keys = bounds[-1]
    slots = key.shape[1]
    places = places_in(plan, form)
    targets = places // group
    here = (iota((n_keys, slots), 0) == key) & live
    marks = jnp.where(here, 1.0, 0.0)
    earlier = iota((slots, slots), 0) < iota((slots, slots), 1)
    rank = jnp.dot(
        marks.astype(jnp.bfloat16),
        jnp.where(earlier, 1.0, 0.0).astype(jnp.bfloat16),
        preferred_element_type=jnp.float32,
    )
    count = jnp.sum(marks, axis=1, keepdims=True).astype(jnp.int32)
    groups = lax.div(count + (group - 1), group)
    lower = iota((n_keys, n_keys), 1) < iota((n_keys, n_keys), 0)
    start = jnp.dot(
        jnp.where(lower, 1.0, 0.0).astype(jnp.bfloat16),
        jnp.broadcast_to(groups, (n_keys, 128)).astype(jnp.bfloat16),
        preferred_element_type=jnp.float32,
    )[:, :1].astype(jnp.int32)
    name = iota((n_keys, 1), 0)
    done = turns = jnp.zeros((1, 1), jnp.int32)
    ends = []
    for lo, hi in zip(bounds, bounds[1:]):
        inside = (name >= lo) & (name < hi)
        start = start + jnp.where(inside, turns * unroll - done, 0)
        here_now = jnp.sum(jnp.where(inside, groups, 0), axis=0, keepdims=True)
        done = done + here_now
        turns = turns + lax.div(here_now + (unroll - 1), unroll)
        ends.append(turns)
    place = jnp.where(here, rank.astype(jnp.int32) + start * group, 0)
    place = jnp.where(live, jnp.sum(place, axis=0, keepdims=True), -1)
    hit = iota((places, slots), 0) == place
    hit = jnp.where(hit, 1.0, 0.0).astype(jnp.bfloat16)
    row = iota((8, slots), 0)
    ids = iota((8, slots), 1) - slots
    low = ids & 127
    values = jnp.where(row == 1, ids - low, jnp.where(row == 2, other, 0))
    values = jnp.where(row == 0, low, values)
    found = lax.dot_general(
        values.astype(jnp.float32).astype(jnp.bfloat16),
        hit,
        (((1,), (1,)), ((), ())),
        preferred_element_type=jnp.float32,
    ).astype(jnp.int32)
    at = iota((n_keys, targets), 1)
    inside = (start <= at) & (at < start + groups)
    names = iota((n_keys, targets), 0)
    base = jnp.zeros_like(names)
    for lo in bounds[1:-1]:
        base = jnp.where(names >= lo, lo, base)
    names = names - base
    tile = found[0:1] + found[1:2] + slots
    plan[0:1, 0:places] = tile + (found[2:3] << SHIFT)
    plan[0:1, places : places + targets] = jnp.sum(
        jnp.where(inside, names, 0), axis=0, keepdims=True
    )
    lane = iota((1, 128), 1)
    last = jnp.zeros((1, 128), jnp.int32)
    for n, end in enumerate(ends):
        last = jnp.where(lane == n + 1, end, last)
    plan[0:1, places + targets :] = last


def around(parts):
    return (parts[0] + parts[2]) + (parts[1] + parts[3])


def divided(value, by, most):
    return sum(jnp.where(value >= by * t, 1, 0) for t in range(1, most // by + 1))


def plan_kernel(
    sizes, where, count, rows, cols, tiles, plan_f, plan_b, held, row_in, col_in, sem
):
    lo, hi = chunks_of(count, tiles, 0)

    copies = [
        pltpu.make_async_copy(rows, row_in, sem.at[0]),
        pltpu.make_async_copy(cols, col_in, sem.at[1]),
    ]
    for copy in copies:
        copy.start()

    @pl.loop(lo, hi)
    def _(i):
        chunk_copy(tiles, held, sem.at[2], i).start()

    held[tiles.shape[0]] = jnp.zeros((BS, BS), jnp.bfloat16)
    for copy in copies:
        copy.wait()
    own_blocks, row_blocks, col_blocks = sizes
    core, x, zl, y, zh = [where[i] for i in range(5)]
    row, col = row_in[...], col_in[...]
    live = iota(row.shape, 1) < count[0, 0]
    owner = divided(col, own_blocks, col_blocks - 1)
    inner = col - owner * own_blocks
    side = (owner & 1) ^ core
    half = col_blocks // 2
    owner = owner >> 1
    turned = ((owner >> 2) ^ zl) * 4 + ((x - (owner & 3)) & 3)
    spot = side * half + turned * own_blocks + inner
    ahead = ((owner & 3) - x) & 3
    order = (1 - ((owner >> 2) ^ zl)) * 4 + ahead
    dest = (1 - side) * half + order * own_blocks + inner

    owner = divided(row, own_blocks, row_blocks - 1)
    inner = row - owner * own_blocks
    away = (owner >> 2) ^ zh
    each = row_blocks // 4
    later = jnp.where(iota(row.shape, 1) >= row.shape[1] // 2, 1, 0)
    turn = jnp.where(away == 1, later, 2)
    key = (turn * 4 + (((owner & 3) - y) & 3)) * own_blocks + inner
    make_plan(key, forward_bounds(sizes), spot, live, FORWARD, plan_f)
    behind = (y - (owner & 3)) & 3
    spot = (behind & 1) * each + away * own_blocks + inner
    key = dest + jnp.where(behind >= 2, col_blocks, 0)
    make_plan(key, backward_bounds(sizes), spot, live, BACKWARD, plan_b)

    @pl.loop(lo, hi)
    def _(i):
        chunk_copy(tiles, held, sem.at[2], i).wait()


def forward_bounds(sizes):
    each = sizes[1] // 4
    return (0, 2 * each, 4 * each, 6 * each)


def backward_bounds(sizes):
    columns = sizes[2]
    return (0, columns, columns + columns // 2, 2 * columns)


def make_plans(sizes, where, count, rows, cols, tiles):
    slots = rows.shape[1]
    places_f = places_of(slots, forward_bounds(sizes), FORWARD)
    places_b = places_of(slots, backward_bounds(sizes), BACKWARD)
    return pl.pallas_call(
        functools.partial(plan_kernel, sizes),
        out_shape=(
            jax.ShapeDtypeStruct((1, plan_size(places_f, FORWARD)), jnp.int32),
            jax.ShapeDtypeStruct((1, plan_size(places_b, BACKWARD)), jnp.int32),
            pltpu.VMEM((tiles.shape[0] + 1, BS, BS), tiles.dtype),
        ),
        in_specs=[smem()] * 2 + [hbm()] * 3,
        out_specs=(vmem(),) * 3,
        scratch_shapes=[pltpu.VMEM(rows.shape, jnp.int32)] * 2
        + [pltpu.SemaphoreType.DMA((3,))],
        compiler_params=pltpu.CompilerParams(vmem_limit_bytes=LIMIT),
        cost_estimate=pl.CostEstimate(
            flops=0, bytes_accessed=tiles.size, transcendentals=0
        ),
        name="make_plans",
    )(where, count, rows, cols, tiles)


def chunks_of(count, tiles, part):
    most = tiles.shape[0] // CHUNK // 2
    live = lax.div(count[0, 0] + (CHUNK - 1), CHUNK)
    return part * most, jnp.minimum(live, (part + 1) * most)


def chunk_copy(tiles, held, sem, i):
    at = pl.ds(pl.multiple_of(i * CHUNK, CHUNK), CHUNK)
    return pltpu.make_async_copy(tiles.at[at], held.at[at], sem)


def fetch(plan, here, sem):
    copy = pltpu.make_async_copy(plan, here, sem)
    copy.start()
    return copy


def multiply(plan, phases, form, tiles, source, tile_first, total):
    group, unroll = form
    places = places_in(plan, form)
    targets = places // group
    lo, hi = [plan[0, places + targets + phase] for phase in phases]

    @pl.loop(lo, hi)
    def _(turn):
        for u in range(unroll):
            at = turn * unroll + u
            spots = [plan[0, at * group + i] for i in range(group)]
            left = [tiles[spot & ((1 << SHIFT) - 1)] for spot in spots]
            right = [source[spot >> SHIFT] for spot in spots]
            if not tile_first:
                left, right = right, left
            total[plan[0, places + at]] += jnp.dot(
                jnp.concatenate(left, axis=1),
                jnp.concatenate(right, axis=0),
                preferred_element_type=jnp.float32,
            )


def forward_away_kernel(count, packed, tiles, _, *refs):
    blocks, outs, refs = refs[:-10], refs[-10:-6], refs[-6:]
    held, feats, plan, plan_sem, total, sem = refs
    coming = fetch(packed, plan, plan_sem)
    lo, hi = chunks_of(count, tiles, 1)

    @pl.loop(lo, hi)
    def _(i):
        chunk_copy(tiles, held, sem, i).start()

    each = blocks[0].shape[0]
    for n, block in enumerate(blocks):
        feats[n * each : (n + 1) * each] = block[...]
    total[...] = jnp.zeros_like(total)

    coming.wait()
    multiply(plan, (0, 1), FORWARD, held, feats, True, total)

    @pl.loop(lo, hi)
    def _(i):
        chunk_copy(tiles, held, sem, i).wait()

    multiply(plan, (1, 2), FORWARD, held, feats, True, total)
    for n, out in enumerate(outs):
        out[...] = total[n * out.shape[0] : (n + 1) * out.shape[0]].astype(out.dtype)


def forward_here_kernel(packed, held, feats, *refs):
    outs, (plan, sem, total) = refs[:4], refs[4:]
    coming = fetch(packed, plan, sem)
    total[...] = jnp.zeros_like(total)
    coming.wait()
    multiply(plan, (2, 3), FORWARD, held, feats, True, total)
    for n, out in enumerate(outs):
        out[...] = total[n * out.shape[0] : (n + 1) * out.shape[0]].astype(out.dtype)


def put_sources(source, first, second):
    each = source.shape[0] // 2
    source[0:each] = first[0:each]
    source[each : 2 * each] = second[0:each]


def backward_near_kernel(packed, held, first, second, total, plan, sem, source):
    coming = fetch(packed, plan, sem)
    put_sources(source, first, second)
    total[...] = jnp.zeros_like(total)
    coming.wait()
    multiply(plan, (0, 1), BACKWARD, held, source, False, total)


def backward_sib_kernel(
    packed, held, first, second, before, near, next_, out, both, plan, sem, source, total
):
    coming = fetch(packed, plan, sem)
    put_sources(source, first, second)
    each = source.shape[0] // 2
    parts = [block[each:].astype(jnp.float32) for block in (near, next_, first, second)]
    both[...] = around(parts).astype(jnp.bfloat16)
    total[...] = before[0 : total.shape[0]]
    coming.wait()
    multiply(plan, (1, 2), BACKWARD, held, source, False, total)
    out[...] = total[...].astype(jnp.bfloat16)


def backward_own_kernel(
    packed, held, first, second, before, out, plan, sem, source, total
):
    coming = fetch(packed, plan, sem)
    put_sources(source, first, second)
    half = total.shape[0]
    total[...] = before[half : 2 * half]
    coming.wait()
    multiply(plan, (2, 3), BACKWARD, held, source, False, total)
    out[...] = total[...].astype(jnp.bfloat16)


def add_kernel(first, second, third, fourth, send):
    parts = [part[...].astype(jnp.float32) for part in (first, second, third, fourth)]
    send[...] = sum(parts).astype(jnp.bfloat16)


def collect_kernel(own, other, send):
    each = send.shape[0] - own.shape[0]
    send[0:each] = own[0:each]
    send[each : 2 * each] = other[0:each]
    grad = own[each:].astype(jnp.float32) + other[each:].astype(jnp.float32)
    send[2 * each :] = grad.astype(jnp.bfloat16)


def kernel_call(kernel, name, outs, n_smem, *args, scratch=(), aliases={}, in_hbm=()):
    specs = [smem() if n < n_smem else vmem() for n in range(len(args))]
    specs = [hbm() if n in in_hbm else spec for n, spec in enumerate(specs)]
    return pl.pallas_call(
        kernel,
        out_shape=tuple(outs),
        in_specs=specs,
        out_specs=(vmem(),) * len(outs),
        scratch_shapes=list(scratch),
        input_output_aliases=aliases,
        compiler_params=pltpu.CompilerParams(vmem_limit_bytes=LIMIT),
        cost_estimate=SMALL,
        name=name,
    )(*args)


def of_blocks(n, dtype=jnp.bfloat16):
    return jax.ShapeDtypeStruct((n, BS, BS), dtype)


def plan_space(plan):
    return [pltpu.SMEM(plan.shape, jnp.int32), pltpu.SemaphoreType.DMA]


def sums(n):
    return pltpu.VMEM((n, BS, BS), jnp.float32)


def middle_kernel(weight, cot, *refs):
    parts, (hidden, send) = refs[:-2], refs[-2:]
    agg = sum(part[...].astype(jnp.float32) for part in parts).astype(jnp.bfloat16)
    w = weight[...]
    pre = jnp.dot(agg, w, preferred_element_type=jnp.float32)
    scale = 0.7978845608028654
    inner = scale * (pre + 0.044715 * (pre * pre * pre))
    t = jnp.tanh(inner)
    half = 0.5 * (1.0 + t)
    hidden[...] = (pre * half).astype(jnp.bfloat16)
    slope = half + 0.5 * pre * (1.0 - t * t) * (
        scale * (1.0 + (3 * 0.044715) * (pre * pre))
    )
    delta = (cot[...].astype(jnp.float32) * slope).astype(jnp.bfloat16)
    grad = lax.dot_general(
        agg, delta, (((0,), (0,)), ((), ())), preferred_element_type=jnp.float32
    ).astype(jnp.bfloat16)
    each = agg.shape[0] // BS
    for j in range(each):
        send[j] = lax.dot_general(
            w,
            delta[j * BS : (j + 1) * BS],
            (((1,), (1,)), ((), ())),
            preferred_element_type=jnp.float32,
        ).astype(jnp.bfloat16)
    for i in range(grad.shape[1] // BS):
        send[each + i] = grad[:, i * BS : (i + 1) * BS]


def pair_kernel(own, sib, grad, other_grad, *sends):
    both = grad[...].astype(jnp.float32) + other_grad[...].astype(jnp.float32)
    each = own.shape[0] // len(sends)
    for n, send in enumerate(sends):
        at = slice(n * each, (n + 1) * each)
        total = own[at].astype(jnp.float32) + sib[at].astype(jnp.float32)
        send[0:each] = total.astype(jnp.bfloat16)
        if n < len(sends) // 2:
            send[each:] = both.astype(jnp.bfloat16)


def gather_kernel(first, second, third, fourth, send):
    parts = (first, second, third, fourth)
    send[...] = around([part[...].astype(jnp.float32) for part in parts]).astype(
        jnp.bfloat16
    )


def last_kernel(send, got, first, second, third, fourth, grad_features, grad_weight):
    parts = (first, second, third, fourth)
    each = first.shape[0]
    for j in range(each):
        total = around([part[j].astype(jnp.float32) for part in parts])
        total = total + got[j].astype(jnp.float32)
        grad_features[j * BS : (j + 1) * BS] = total.T.astype(jnp.bfloat16)
    for i in range(grad_weight.shape[1] // BS):
        total = send[each + i].astype(jnp.float32) + got[each + i].astype(jnp.float32)
        grad_weight[:, i * BS : (i + 1) * BS] = total


def swap_core(value):
    return shift(value, "core", 1)


def shift(value, axis, by):
    n = lax.axis_size(axis)
    return lax.ppermute(value, axis, [(i, (i + by) % n) for i in range(n)])


def local(features, weight, tile_values, tile_rows, tile_cols, tile_count, cotangent):
    f_in, f_hid = weight.shape
    nodes = features.shape[0]
    own_blocks = nodes // BS
    n_x, n_zl = lax.axis_size("x"), lax.axis_size("zl")
    n_col = lax.axis_size(COL)
    n_half = n_x * n_zl
    row_blocks = own_blocks * n_col
    col_blocks = own_blocks * n_half * 2
    tiles = pltpu.with_memory_space_constraint(tile_values[0, 0], pltpu.HBM)
    sent_blocks = own_blocks + f_in * f_hid // (BS * BS)
    sizes = (own_blocks, row_blocks, col_blocks)
    rows = pltpu.with_memory_space_constraint(tile_rows[0], pltpu.HBM)
    cols = pltpu.with_memory_space_constraint(tile_cols[0], pltpu.HBM)
    where = jnp.stack([lax.axis_index(a) for a in ("core", "x", "zl", "y", "zh")])

    near = [features] + [shift(features, "x", by) for by in range(1, n_x)]
    far = [shift(features, "zl", 1)]
    plan_f, plan_b, held = make_plans(sizes, where, tile_count, rows, cols, tiles)
    near, far, held = lax.optimization_barrier((near, far, held))
    far += [shift(near[1], "zl", 1), shift(far[0], "x", 2), shift(near[3], "zl", 1)]
    other = [swap_core(block) for block in near + far]
    blocks = [b.reshape(own_blocks, BS, f_in) for b in near + far + other]

    each = row_blocks // 4
    *sends, held, feats = kernel_call(
        forward_away_kernel,
        "forward_away",
        [of_blocks(own_blocks, jnp.float32)]
        + [of_blocks(own_blocks)] * 3
        + [pltpu.VMEM(held.shape, held.dtype), of_blocks(col_blocks)],
        1,
        tile_count,
        plan_f,
        tiles,
        held,
        *blocks,
        scratch=plan_space(plan_f) + [sums(2 * each), pltpu.SemaphoreType.DMA],
        aliases={3: 4},
        in_hbm=(2,),
    )
    away = [sends[0]] + [shift(sends[by], "y", by) for by in (1, 2, 3)]
    sends = kernel_call(
        forward_here_kernel,
        "forward_here",
        [of_blocks(own_blocks, jnp.float32)] + [of_blocks(own_blocks)] * 3,
        0,
        plan_f,
        held,
        feats,
        scratch=plan_space(plan_f) + [sums(2 * each)],
    )
    here = [sends[0]] + [shift(sends[by], "y", by) for by in (1, 2, 3)]
    (send,) = kernel_call(add_kernel, "add", [of_blocks(own_blocks)], 0, *away)
    parts = [part.reshape(nodes, f_in) for part in here + [shift(send, "zh", 1)]]
    hidden, send = kernel_call(
        middle_kernel,
        "middle",
        [
            jax.ShapeDtypeStruct((nodes, f_hid), jnp.bfloat16),
            of_blocks(sent_blocks),
        ],
        0,
        weight,
        cotangent,
        *parts,
    )

    (send,) = kernel_call(
        collect_kernel,
        "collect",
        [of_blocks(sent_blocks + own_blocks)],
        0,
        send,
        shift(send, "zh", 1),
    )
    near = [send] + [shift(send, "y", by) for by in (1, 2, 3)]
    (total,) = kernel_call(
        backward_near_kernel,
        "backward_near",
        [of_blocks(col_blocks, jnp.float32)],
        0,
        plan_b,
        held,
        *near[:2],
        scratch=plan_space(plan_b) + [pltpu.VMEM((2 * each, BS, BS), jnp.bfloat16)],
    )
    half = col_blocks // 2
    sib, grad = kernel_call(
        backward_sib_kernel,
        "backward_sib",
        [of_blocks(half), of_blocks(sent_blocks - own_blocks)],
        0,
        plan_b,
        held,
        *near[2:],
        total,
        *near[:2],
        scratch=plan_space(plan_b) + [pltpu.VMEM((2 * each, BS, BS), jnp.bfloat16), sums(half)],
    )
    other_sib, other_grad = swap_core(sib), swap_core(grad)
    (own,) = kernel_call(
        backward_own_kernel,
        "backward_own",
        [of_blocks(half)],
        0,
        plan_b,
        held,
        *near[2:],
        total,
        scratch=plan_space(plan_b) + [pltpu.VMEM((2 * each, BS, BS), jnp.bfloat16), sums(half)],
    )
    other_sib, other_grad, own = lax.optimization_barrier((other_sib, other_grad, own))
    n_grad = sent_blocks - own_blocks
    sends = kernel_call(
        pair_kernel,
        "pair",
        [of_blocks(own_blocks + n_grad)] * 4 + [of_blocks(own_blocks)] * 4,
        0,
        own,
        other_sib,
        grad,
        other_grad,
    )
    away = [sends[0]] + [shift(sends[by], "x", by) for by in (2, 1, 3)]
    here = [sends[4]] + [shift(sends[4 + by], "x", by) for by in (2, 1, 3)]
    away, here[2:] = lax.optimization_barrier((away, here[2:]))
    (send,) = kernel_call(
        gather_kernel,
        "gather",
        [of_blocks(sent_blocks)],
        0,
        away[0],
        away[2],
        away[1],
        away[3],
    )
    grad_features, grad_weight = kernel_call(
        last_kernel,
        "last",
        [
            jax.ShapeDtypeStruct((nodes, f_in), jnp.bfloat16),
            jax.ShapeDtypeStruct((f_in, f_hid), jnp.float32),
        ],
        0,
        send,
        shift(send, "zl", 1),
        here[0],
        here[2],
        here[1],
        here[3],
    )
    return hidden, grad_weight, grad_features


def solution(mesh):
    fine = Mesh(mesh.devices.reshape(2, 4, 2, 2, 4), AXES)
    nodes = P(AXES, None)
    mapped = jax.shard_map(
        local,
        mesh=fine,
        in_specs=(
            nodes,
            P(),
            P(ROW, COL, None, None, None),
            P(ROW, COL, None),
            P(ROW, COL, None),
            P(ROW, COL),
            nodes,
        ),
        out_specs=(nodes, P(), nodes),
        check_vma=False,
    )
    return mapped
```

```python
import functools

import jax
import jax.numpy as jnp
from jax import lax
from jax.experimental import pallas as pl
from jax.experimental.pallas import tpu as pltpu
from jax.sharding import Mesh, PartitionSpec as P

AXES = ("zl", "x", "core", "zh", "y")
ROW = ("zl", "x", "core")
COL = ("zh", "y")
BS = 128
SHIFT = 10
FORWARD = (4, 16)
BACKWARD = (2, 32)
LIMIT = 24 << 20
CHUNK = 16
SMALL = pl.CostEstimate(flops=BS, bytes_accessed=BS, transcendentals=0)


def smem():
    return pl.BlockSpec(memory_space=pltpu.SMEM)


def vmem():
    return pl.BlockSpec(memory_space=pltpu.VMEM)


def hbm():
    return pl.BlockSpec(memory_space=pltpu.HBM)


def iota(shape, dim):
    return lax.broadcasted_iota(jnp.int32, shape, dim)


def places_of(slots, bounds, form):
    group, unroll = form
    groups = (slots + bounds[-1] * (group - 1)) // group
    groups += (len(bounds) - 1) * (unroll - 1)
    return -(-groups // 128) * 128 * group


def plan_size(places, form):
    return places + places // form[0] + 128


def places_in(plan, form):
    group, _ = form
    return (plan.shape[1] - 128) // (group + 1) * group


def make_plan(key, bounds, other, live, form, plan):
    group, unroll = form
    n_keys = bounds[-1]
    slots = key.shape[1]
    places = places_in(plan, form)
    targets = places // group
    here = (iota((n_keys, slots), 0) == key) & live
    marks = jnp.where(here, 1.0, 0.0)
    earlier = iota((slots, slots), 0) < iota((slots, slots), 1)
    rank = jnp.dot(
        marks.astype(jnp.bfloat16),
        jnp.where(earlier, 1.0, 0.0).astype(jnp.bfloat16),
        preferred_element_type=jnp.float32,
    )
    count = jnp.sum(marks, axis=1, keepdims=True).astype(jnp.int32)
    groups = lax.div(count + (group - 1), group)
    lower = iota((n_keys, n_keys), 1) < iota((n_keys, n_keys), 0)
    start = jnp.dot(
        jnp.where(lower, 1.0, 0.0).astype(jnp.bfloat16),
        jnp.broadcast_to(groups, (n_keys, 128)).astype(jnp.bfloat16),
        preferred_element_type=jnp.float32,
    )[:, :1].astype(jnp.int32)
    name = iota((n_keys, 1), 0)
    done = turns = jnp.zeros((1, 1), jnp.int32)
    ends = []
    for lo, hi in zip(bounds, bounds[1:]):
        inside = (name >= lo) & (name < hi)
        start = start + jnp.where(inside, turns * unroll - done, 0)
        here_now = jnp.sum(jnp.where(inside, groups, 0), axis=0, keepdims=True)
        done = done + here_now
        turns = turns + lax.div(here_now + (unroll - 1), unroll)
        ends.append(turns)
    place = jnp.where(here, rank.astype(jnp.int32) + start * group, 0)
    place = jnp.where(live, jnp.sum(place, axis=0, keepdims=True), -1)
    hit = iota((places, slots), 0) == place
    hit = jnp.where(hit, 1.0, 0.0).astype(jnp.bfloat16)
    row = iota((8, slots), 0)
    ids = iota((8, slots), 1) - slots
    low = ids & 127
    values = jnp.where(row == 1, ids - low, jnp.where(row == 2, other, 0))
    values = jnp.where(row == 0, low, values)
    found = lax.dot_general(
        values.astype(jnp.float32).astype(jnp.bfloat16),
        hit,
        (((1,), (1,)), ((), ())),
        preferred_element_type=jnp.float32,
    ).astype(jnp.int32)
    at = iota((n_keys, targets), 1)
    inside = (start <= at) & (at < start + groups)
    names = iota((n_keys, targets), 0)
    base = jnp.zeros_like(names)
    for lo in bounds[1:-1]:
        base = jnp.where(names >= lo, lo, base)
    names = names - base
    tile = found[0:1] + found[1:2] + slots
    plan[0:1, 0:places] = tile + (found[2:3] << SHIFT)
    plan[0:1, places : places + targets] = jnp.sum(
        jnp.where(inside, names, 0), axis=0, keepdims=True
    )
    lane = iota((1, 128), 1)
    last = jnp.zeros((1, 128), jnp.int32)
    for n, end in enumerate(ends):
        last = jnp.where(lane == n + 1, end, last)
    plan[0:1, places + targets :] = last


def around(parts):
    return (parts[0] + parts[2]) + (parts[1] + parts[3])


def divided(value, by, most):
    return sum(jnp.where(value >= by * t, 1, 0) for t in range(1, most // by + 1))


def plan_kernel(
    sizes, where, count, rows, cols, tiles, plan_f, plan_b, held, row_in, col_in, sem
):
    lo, hi = chunks_of(count, tiles, 0)

    copies = [
        pltpu.make_async_copy(rows, row_in, sem.at[0]),
        pltpu.make_async_copy(cols, col_in, sem.at[1]),
    ]
    for copy in copies:
        copy.start()

    @pl.loop(lo, hi)
    def _(i):
        chunk_copy(tiles, held, sem.at[2], i).start()

    held[tiles.shape[0]] = jnp.zeros((BS, BS), jnp.bfloat16)
    for copy in copies:
        copy.wait()
    own_blocks, row_blocks, col_blocks = sizes
    core, x, zl, y, zh = [where[i] for i in range(5)]
    row, col = row_in[...], col_in[...]
    live = iota(row.shape, 1) < count[0, 0]
    owner = divided(col, own_blocks, col_blocks - 1)
    inner = col - owner * own_blocks
    side = (owner & 1) ^ core
    half = col_blocks // 2
    owner = owner >> 1
    turned = ((owner >> 2) ^ zl) * 4 + ((x - (owner & 3)) & 3)
    spot = side * half + turned * own_blocks + inner
    ahead = ((owner & 3) - x) & 3
    order = (1 - ((owner >> 2) ^ zl)) * 4 + ahead
    dest = (1 - side) * half + order * own_blocks + inner

    owner = divided(row, own_blocks, row_blocks - 1)
    inner = row - owner * own_blocks
    away = (owner >> 2) ^ zh
    each = row_blocks // 4
    later = jnp.where(iota(row.shape, 1) >= row.shape[1] // 2, 1, 0)
    turn = jnp.where(away == 1, later, 2)
    key = (turn * 4 + (((owner & 3) - y) & 3)) * own_blocks + inner
    make_plan(key, forward_bounds(sizes), spot, live, FORWARD, plan_f)
    behind = (y - (owner & 3)) & 3
    spot = (behind & 1) * each + away * own_blocks + inner
    key = dest + jnp.where(behind >= 2, col_blocks, 0)
    make_plan(key, backward_bounds(sizes), spot, live, BACKWARD, plan_b)

    @pl.loop(lo, hi)
    def _(i):
        chunk_copy(tiles, held, sem.at[2], i).wait()


def forward_bounds(sizes):
    each = sizes[1] // 4
    return (0, 2 * each, 4 * each, 6 * each)


def backward_bounds(sizes):
    columns = sizes[2]
    return (0, columns, columns + columns // 2, 2 * columns)


def make_plans(sizes, where, count, rows, cols, tiles):
    slots = rows.shape[1]
    places_f = places_of(slots, forward_bounds(sizes), FORWARD)
    places_b = places_of(slots, backward_bounds(sizes), BACKWARD)
    return pl.pallas_call(
        functools.partial(plan_kernel, sizes),
        out_shape=(
            jax.ShapeDtypeStruct((1, plan_size(places_f, FORWARD)), jnp.int32),
            jax.ShapeDtypeStruct((1, plan_size(places_b, BACKWARD)), jnp.int32),
            pltpu.VMEM((tiles.shape[0] + 1, BS, BS), tiles.dtype),
        ),
        in_specs=[smem()] * 2 + [hbm()] * 3,
        out_specs=(vmem(),) * 3,
        scratch_shapes=[pltpu.VMEM(rows.shape, jnp.int32)] * 2
        + [pltpu.SemaphoreType.DMA((3,))],
        compiler_params=pltpu.CompilerParams(vmem_limit_bytes=LIMIT),
        cost_estimate=pl.CostEstimate(
            flops=0, bytes_accessed=tiles.size, transcendentals=0
        ),
        name="make_plans",
    )(where, count, rows, cols, tiles)


def chunks_of(count, tiles, part):
    most = tiles.shape[0] // CHUNK // 2
    live = lax.div(count[0, 0] + (CHUNK - 1), CHUNK)
    return part * most, jnp.minimum(live, (part + 1) * most)


def chunk_copy(tiles, held, sem, i):
    at = pl.ds(pl.multiple_of(i * CHUNK, CHUNK), CHUNK)
    return pltpu.make_async_copy(tiles.at[at], held.at[at], sem)


def fetch(plan, here, sem):
    copy = pltpu.make_async_copy(plan, here, sem)
    copy.start()
    return copy


def multiply(plan, phases, form, tiles, source, tile_first, total):
    group, unroll = form
    places = places_in(plan, form)
    targets = places // group
    lo, hi = [plan[0, places + targets + phase] for phase in phases]

    @pl.loop(lo, hi)
    def _(turn):
        for u in range(unroll):
            at = turn * unroll + u
            spots = [plan[0, at * group + i] for i in range(group)]
            left = [tiles[spot & ((1 << SHIFT) - 1)] for spot in spots]
            right = [source[spot >> SHIFT] for spot in spots]
            if not tile_first:
                left, right = right, left
            total[plan[0, places + at]] += jnp.dot(
                jnp.concatenate(left, axis=1),
                jnp.concatenate(right, axis=0),
                preferred_element_type=jnp.float32,
            )


def forward_away_kernel(count, packed, tiles, _, *refs):
    blocks, outs, refs = refs[:-10], refs[-10:-6], refs[-6:]
    held, feats, plan, plan_sem, total, sem = refs
    coming = fetch(packed, plan, plan_sem)
    lo, hi = chunks_of(count, tiles, 1)

    @pl.loop(lo, hi)
    def _(i):
        chunk_copy(tiles, held, sem, i).start()

    each = blocks[0].shape[0]
    for n, block in enumerate(blocks):
        feats[n * each : (n + 1) * each] = block[...]
    total[...] = jnp.zeros_like(total)

    coming.wait()
    multiply(plan, (0, 1), FORWARD, held, feats, True, total)

    @pl.loop(lo, hi)
    def _(i):
        chunk_copy(tiles, held, sem, i).wait()

    multiply(plan, (1, 2), FORWARD, held, feats, True, total)
    for n, out in enumerate(outs):
        out[...] = total[n * out.shape[0] : (n + 1) * out.shape[0]].astype(out.dtype)


def forward_here_kernel(packed, held, feats, *refs):
    outs, (plan, sem, total) = refs[:4], refs[4:]
    coming = fetch(packed, plan, sem)
    total[...] = jnp.zeros_like(total)
    coming.wait()
    multiply(plan, (2, 3), FORWARD, held, feats, True, total)
    for n, out in enumerate(outs):
        out[...] = total[n * out.shape[0] : (n + 1) * out.shape[0]].astype(out.dtype)


def put_sources(source, first, second):
    each = source.shape[0] // 2
    source[0:each] = first[0:each]
    source[each : 2 * each] = second[0:each]


def backward_near_kernel(packed, held, first, second, total, plan, sem, source):
    coming = fetch(packed, plan, sem)
    put_sources(source, first, second)
    total[...] = jnp.zeros_like(total)
    coming.wait()
    multiply(plan, (0, 1), BACKWARD, held, source, False, total)


def backward_sib_kernel(
    packed, held, first, second, before, near, next_, out, both, plan, sem, source, total
):
    coming = fetch(packed, plan, sem)
    put_sources(source, first, second)
    each = source.shape[0] // 2
    parts = [block[each:].astype(jnp.float32) for block in (near, next_, first, second)]
    both[...] = around(parts).astype(jnp.bfloat16)
    total[...] = before[0 : total.shape[0]]
    coming.wait()
    multiply(plan, (1, 2), BACKWARD, held, source, False, total)
    out[...] = total[...].astype(jnp.bfloat16)


def backward_own_kernel(
    packed, held, first, second, before, out, plan, sem, source, total
):
    coming = fetch(packed, plan, sem)
    put_sources(source, first, second)
    half = total.shape[0]
    total[...] = before[half : 2 * half]
    coming.wait()
    multiply(plan, (2, 3), BACKWARD, held, source, False, total)
    out[...] = total[...].astype(jnp.bfloat16)


def add_kernel(first, second, third, fourth, send):
    parts = [part[...].astype(jnp.float32) for part in (first, second, third, fourth)]
    send[...] = sum(parts).astype(jnp.bfloat16)


def collect_kernel(own, other, send):
    each = send.shape[0] - own.shape[0]
    send[0:each] = own[0:each]
    send[each : 2 * each] = other[0:each]
    grad = own[each:].astype(jnp.float32) + other[each:].astype(jnp.float32)
    send[2 * each :] = grad.astype(jnp.bfloat16)


def kernel_call(kernel, name, outs, n_smem, *args, scratch=(), aliases={}, in_hbm=()):
    specs = [smem() if n < n_smem else vmem() for n in range(len(args))]
    specs = [hbm() if n in in_hbm else spec for n, spec in enumerate(specs)]
    return pl.pallas_call(
        kernel,
        out_shape=tuple(outs),
        in_specs=specs,
        out_specs=(vmem(),) * len(outs),
        scratch_shapes=list(scratch),
        input_output_aliases=aliases,
        compiler_params=pltpu.CompilerParams(vmem_limit_bytes=LIMIT),
        cost_estimate=SMALL,
        name=name,
    )(*args)


def of_blocks(n, dtype=jnp.bfloat16):
    return jax.ShapeDtypeStruct((n, BS, BS), dtype)


def plan_space(plan):
    return [pltpu.SMEM(plan.shape, jnp.int32), pltpu.SemaphoreType.DMA]


def sums(n):
    return pltpu.VMEM((n, BS, BS), jnp.float32)


def middle_kernel(weight, cot, *refs):
    parts, (hidden, send) = refs[:-2], refs[-2:]
    agg = sum(part[...].astype(jnp.float32) for part in parts).astype(jnp.bfloat16)
    w = weight[...]
    pre = jnp.dot(agg, w, preferred_element_type=jnp.float32)
    scale = 0.7978845608028654
    inner = scale * (pre + 0.044715 * (pre * pre * pre))
    t = jnp.tanh(inner)
    half = 0.5 * (1.0 + t)
    hidden[...] = (pre * half).astype(jnp.bfloat16)
    slope = half + 0.5 * pre * (1.0 - t * t) * (
        scale * (1.0 + (3 * 0.044715) * (pre * pre))
    )
    delta = (cot[...].astype(jnp.float32) * slope).astype(jnp.bfloat16)
    grad = lax.dot_general(
        agg, delta, (((0,), (0,)), ((), ())), preferred_element_type=jnp.float32
    ).astype(jnp.bfloat16)
    each = agg.shape[0] // BS
    for j in range(each):
        send[j] = lax.dot_general(
            w,
            delta[j * BS : (j + 1) * BS],
            (((1,), (1,)), ((), ())),
            preferred_element_type=jnp.float32,
        ).astype(jnp.bfloat16)
    for i in range(grad.shape[1] // BS):
        send[each + i] = grad[:, i * BS : (i + 1) * BS]


def pair_kernel(own, sib, grad, other_grad, *sends):
    both = grad[...].astype(jnp.float32) + other_grad[...].astype(jnp.float32)
    each = own.shape[0] // len(sends)
    for n, send in enumerate(sends):
        at = slice(n * each, (n + 1) * each)
        total = own[at].astype(jnp.float32) + sib[at].astype(jnp.float32)
        send[0:each] = total.astype(jnp.bfloat16)
        if n < len(sends) // 2:
            send[each:] = both.astype(jnp.bfloat16)


def gather_kernel(first, second, third, fourth, send):
    parts = (first, second, third, fourth)
    send[...] = around([part[...].astype(jnp.float32) for part in parts]).astype(
        jnp.bfloat16
    )


def last_kernel(send, got, first, second, third, fourth, grad_features, grad_weight):
    parts = (first, second, third, fourth)
    each = first.shape[0]
    for j in range(each):
        total = around([part[j].astype(jnp.float32) for part in parts])
        total = total + got[j].astype(jnp.float32)
        grad_features[j * BS : (j + 1) * BS] = total.T.astype(jnp.bfloat16)
    for i in range(grad_weight.shape[1] // BS):
        total = send[each + i].astype(jnp.float32) + got[each + i].astype(jnp.float32)
        grad_weight[:, i * BS : (i + 1) * BS] = total


def swap_core(value):
    return shift(value, "core", 1)


def shift(value, axis, by):
    n = lax.axis_size(axis)
    return lax.ppermute(value, axis, [(i, (i + by) % n) for i in range(n)])


def local(features, weight, tile_values, tile_rows, tile_cols, tile_count, cotangent):
    f_in, f_hid = weight.shape
    nodes = features.shape[0]
    own_blocks = nodes // BS
    n_x, n_zl = lax.axis_size("x"), lax.axis_size("zl")
    n_col = lax.axis_size(COL)
    n_half = n_x * n_zl
    row_blocks = own_blocks * n_col
    col_blocks = own_blocks * n_half * 2
    tiles = pltpu.with_memory_space_constraint(tile_values[0, 0], pltpu.HBM)
    sent_blocks = own_blocks + f_in * f_hid // (BS * BS)
    sizes = (own_blocks, row_blocks, col_blocks)
    rows = pltpu.with_memory_space_constraint(tile_rows[0], pltpu.HBM)
    cols = pltpu.with_memory_space_constraint(tile_cols[0], pltpu.HBM)
    where = jnp.stack([lax.axis_index(a) for a in ("core", "x", "zl", "y", "zh")])

    near = [features] + [shift(features, "x", by) for by in range(1, n_x)]
    far = [shift(features, "zl", 1)]
    plan_f, plan_b, held = make_plans(sizes, where, tile_count, rows, cols, tiles)
    near, far, held = lax.optimization_barrier((near, far, held))
    far += [shift(near[1], "zl", 1), shift(far[0], "x", 2), shift(near[3], "zl", 1)]
    other = [swap_core(block) for block in near + far]
    blocks = [b.reshape(own_blocks, BS, f_in) for b in near + far + other]

    each = row_blocks // 4
    *sends, held, feats = kernel_call(
        forward_away_kernel,
        "forward_away",
        [of_blocks(own_blocks, jnp.float32)]
        + [of_blocks(own_blocks)] * 3
        + [pltpu.VMEM(held.shape, held.dtype), of_blocks(col_blocks)],
        1,
        tile_count,
        plan_f,
        tiles,
        held,
        *blocks,
        scratch=plan_space(plan_f) + [sums(2 * each), pltpu.SemaphoreType.DMA],
        aliases={3: 4},
        in_hbm=(2,),
    )
    away = [sends[0]] + [shift(sends[by], "y", by) for by in (1, 2, 3)]
    sends = kernel_call(
        forward_here_kernel,
        "forward_here",
        [of_blocks(own_blocks, jnp.float32)] + [of_blocks(own_blocks)] * 3,
        0,
        plan_f,
        held,
        feats,
        scratch=plan_space(plan_f) + [sums(2 * each)],
    )
    here = [sends[0]] + [shift(sends[by], "y", by) for by in (1, 2, 3)]
    (send,) = kernel_call(add_kernel, "add", [of_blocks(own_blocks)], 0, *away)
    parts = [part.reshape(nodes, f_in) for part in here + [shift(send, "zh", 1)]]
    hidden, send = kernel_call(
        middle_kernel,
        "middle",
        [
            jax.ShapeDtypeStruct((nodes, f_hid), jnp.bfloat16),
            of_blocks(sent_blocks),
        ],
        0,
        weight,
        cotangent,
        *parts,
    )

    (send,) = kernel_call(
        collect_kernel,
        "collect",
        [of_blocks(sent_blocks + own_blocks)],
        0,
        send,
        shift(send, "zh", 1),
    )
    near = [send] + [shift(send, "y", by) for by in (1, 2, 3)]
    (total,) = kernel_call(
        backward_near_kernel,
        "backward_near",
        [of_blocks(col_blocks, jnp.float32)],
        0,
        plan_b,
        held,
        *near[:2],
        scratch=plan_space(plan_b) + [pltpu.VMEM((2 * each, BS, BS), jnp.bfloat16)],
    )
    half = col_blocks // 2
    sib, grad = kernel_call(
        backward_sib_kernel,
        "backward_sib",
        [of_blocks(half), of_blocks(sent_blocks - own_blocks)],
        0,
        plan_b,
        held,
        *near[2:],
        total,
        *near[:2],
        scratch=plan_space(plan_b) + [pltpu.VMEM((2 * each, BS, BS), jnp.bfloat16), sums(half)],
    )
    other_sib, other_grad = swap_core(sib), swap_core(grad)
    (own,) = kernel_call(
        backward_own_kernel,
        "backward_own",
        [of_blocks(half)],
        0,
        plan_b,
        held,
        *near[2:],
        total,
        scratch=plan_space(plan_b) + [pltpu.VMEM((2 * each, BS, BS), jnp.bfloat16), sums(half)],
    )
    other_sib, other_grad, own = lax.optimization_barrier((other_sib, other_grad, own))
    n_grad = sent_blocks - own_blocks
    sends = kernel_call(
        pair_kernel,
        "pair",
        [of_blocks(own_blocks + n_grad)] * 4 + [of_blocks(own_blocks)] * 4,
        0,
        own,
        other_sib,
        grad,
        other_grad,
    )
    away = [sends[0]] + [shift(sends[by], "x", by) for by in (2, 1, 3)]
    here = [sends[4]] + [shift(sends[4 + by], "x", by) for by in (2, 1, 3)]
    away, here[2:] = lax.optimization_barrier((away, here[2:]))
    (send,) = kernel_call(
        gather_kernel,
        "gather",
        [of_blocks(sent_blocks)],
        0,
        away[0],
        away[2],
        away[1],
        away[3],
    )
    grad_features, grad_weight = kernel_call(
        last_kernel,
        "last",
        [
            jax.ShapeDtypeStruct((nodes, f_in), jnp.bfloat16),
            jax.ShapeDtypeStruct((f_in, f_hid), jnp.float32),
        ],
        0,
        send,
        shift(send, "zl", 1),
        here[0],
        here[2],
        here[1],
        here[3],
    )
    return hidden, grad_weight, grad_features


def solution(mesh):
    fine = Mesh(mesh.devices.reshape(2, 4, 2, 2, 4), AXES)
    nodes = P(AXES, None)
    mapped = jax.shard_map(
        local,
        mesh=fine,
        in_specs=(
            nodes,
            P(),
            P(ROW, COL, None, None, None),
            P(ROW, COL, None),
            P(ROW, COL, None),
            P(ROW, COL),
            nodes,
        ),
        out_specs=(nodes, P(), nodes),
        check_vma=False,
    )
    return mapped
```
